256 devices in a mesh: gx: 4 (over z_lo), gy: 8 (over x, core), gz: 8 (over z_hi, y).
Axes of the slice: x: 4, y: 4, z: 8 (z_hi: 2, z_lo: 4; z = z_hi * 4 + z_lo), core: 2. Of those that a mesh axis runs over, the one named last changes fastest.
Arguments:
- tokens: bfloat16 [512, 12288], P('gz', 'gx'), may hold values from -6 to 6
- grad_out: bfloat16 [512, 12288], P('gz', 'gx'), may hold values from -6 to 6
- w_in: bfloat16 [12288, 24576], P('gx', ('gy', 'gz')), may hold values from -0.0546875 to 0.0546875
- w_out: bfloat16 [24576, 12288], P(('gy', 'gz'), 'gx'), may hold values from -0.0546875 to 0.0546875
Outputs:
- grad_tokens: bfloat16 [512, 12288], P(('gy', 'gz'), 'gx')
- grad_w_in: bfloat16 [12288, 24576], P('gx', ('gy', 'gz'))
- grad_w_out: bfloat16 [24576, 12288], P(('gy', 'gz'), 'gx')
The draws below stay inside these ranges and needn't reach their ends.
All inputs are finite; a program needn't handle non-finite values.
Results may differ from the reference program's by a relative error of at most 0.0049.
Values may be sent and summed in bfloat16 or wider, within the bound.
A program may use at most 64 MiB of HBM per device.

```python
import jax
import jax.numpy as jnp
from jax import lax

D = 12288
FF = 24576
TOKENS = 512


def shard_levels(stream_key, dims, shards, least, high):
    gain, own = 1.0, jax.random.fold_in(stream_key, 6)
    for dim, parts in shards:
        draws = jnp.exp(jax.random.uniform(jax.random.fold_in(own, dim), (parts,), jnp.float32, least / len(shards), high / len(shards)))
        gain = gain * jnp.repeat(draws, dims[dim] // parts).reshape([-1 if axis == dim else 1 for axis in range(len(dims))])
    return gain


def bell_draw(stream_key, dims, deviation, reach, split=(), dtype=jnp.bfloat16):
    entries = deviation * jax.random.normal(stream_key, dims, jnp.float32)
    if split:
        entries = entries * shard_levels(stream_key, dims, split, -0.22, 0.18)
    return jnp.clip(entries, -reach, reach).astype(dtype)


def setup_inputs(seed: int = 0) -> dict:
    seeds = jax.random.split(jax.random.key(seed), 5)
    tokens = bell_draw(seeds[0], (TOKENS, D), 1.0, 6.0, ((0, 8), (1, 4)))
    grad_out = bell_draw(seeds[1], (TOKENS, D), 1.0, 6.0, ((0, 8), (1, 4)))
    w_in = bell_draw(seeds[2], (D, FF), D ** -0.5, 0.0546875, ((0, 4), (1, 64)))
    w_out = bell_draw(seeds[3], (FF, D), D ** -0.5, 0.0546875, ((0, 64), (1, 4)))
    return dict(tokens=tokens, grad_out=grad_out, w_in=w_in, w_out=w_out)


coef = 0.7978845608028654


def gelu_pair(pre, back):
    inner = coef * (pre + 0.044715 * pre * pre * pre)
    tval = jnp.tanh(inner)
    act = 0.5 * pre * (1.0 + tval)
    slope = 0.5 * (1.0 + tval) + 0.5 * pre * (1.0 - tval * tval) * coef * (1.0 + 3.0 * 0.044715 * pre * pre)
    return act.astype(jnp.bfloat16), (back * slope).astype(jnp.bfloat16)


def reference(tokens, grad_out, w_in, w_out):
    pre = jnp.dot(tokens, w_in, preferred_element_type=jnp.float32)
    back = lax.dot_general(grad_out, w_out, (((1,), (1,)), ((), ())), preferred_element_type=jnp.float32)
    act, dpre = gelu_pair(pre, back)
    grad_w_out = lax.dot_general(act, grad_out, (((0,), (0,)), ((), ())), preferred_element_type=jnp.float32).astype(jnp.bfloat16)
    grad_w_in = lax.dot_general(tokens, dpre, (((0,), (0,)), ((), ())), preferred_element_type=jnp.float32).astype(jnp.bfloat16)
    grad_tokens = lax.dot_general(dpre, w_in, (((1,), (1,)), ((), ())), preferred_element_type=jnp.float32).astype(jnp.bfloat16)
    return grad_tokens, grad_w_in, grad_w_out
```

```python
import functools

import jax
import jax.numpy as jnp
from jax import lax
from jax.experimental import pallas as pl
from jax.experimental.pallas import tpu as pltpu
from jax.sharding import PartitionSpec as P

MESH = pl.DeviceIdType.MESH
F32, BF16 = jnp.float32, jnp.bfloat16
coef = 0.7978845608028654
NN = (((1,), (0,)), ((), ()))
NT = (((1,), (1,)), ((), ()))
TN = (((0,), (0,)), ((), ()))

FEAT, HID, TOK = 3072, 384, 512
HALF = FEAT // 2
P2O, P2P = 512, 768
N_SEMS = 128


def gelu_pair(pre, back):
    inner = coef * (pre + 0.044715 * pre * pre * pre)
    tval = jnp.tanh(inner)
    act = 0.5 * pre * (1.0 + tval)
    slope = 0.5 * (1.0 + tval) + 0.5 * pre * (1.0 - tval * tval) * coef * (
        1.0 + 3.0 * 0.044715 * pre * pre
    )
    return act.astype(BF16), (back * slope).astype(BF16)


def dot(a, b, dims):
    return lax.dot_general(a, b, dims, preferred_element_type=F32)


def kernel(
    tok_hbm, dy_hbm, win_hbm, wout_hbm,
    gt_ref, gwi_hbm, gwo_hbm,
    both, win, wout, win_sib, part, part16, inbox, acts, dpre_sib,
    quad, ysend, yrecv, xsend, xrecv, own, fin_send, fin_recv, gwi, gwo,
    ssem, rsem, xs_sem, xr_sem, lsem,
):
    gx, gy, gz = lax.axis_index("gx"), lax.axis_index("gy"), lax.axis_index("gz")
    x, c, y, h, l = gy // 2, gy % 2, gz % 4, gz // 4, gx

    def at(x=x, c=c, y=y, h=h, l=l):
        return (l, x * 2 + c, h * 4 + y)

    def turn(v, d):
        return (v + d + 4) % 4

    l1, l2, l3 = l + 1 - 2 * (l % 2), turn(l, 2), 3 - l
    lane = {1: l1, 2: l2, 3: l3}

    mine = pl.multiple_of(gz * 64, 64)
    loads = [
        pltpu.make_async_copy(tok_hbm, both.at[0, pl.ds(mine, 64)], lsem.at[0]),
        pltpu.make_async_copy(dy_hbm, both.at[1, pl.ds(mine, 64)], lsem.at[1]),
        pltpu.make_async_copy(win_hbm, win, lsem.at[2]),
        pltpu.make_async_copy(wout_hbm, wout, lsem.at[3]),
    ]
    for cp in loads:
        cp.start()

    peers = (
        [at(x=turn(x, d)) for d in (1, 2, 3)]
        + [at(y=turn(y, d)) for d in (1, 2, 3)]
        + [at(l=lane[j]) for j in (1, 2, 3)]
        + [at(h=1 - h), at(h=1 - h, c=1 - c), at(c=1 - c)]
    )
    barrier = pltpu.get_barrier_semaphore()
    for peer in peers:
        pl.semaphore_signal(barrier, inc=1, device_id=peer, device_id_type=MESH)
    pl.semaphore_wait(barrier, len(peers))

    sent = []

    def send(src, dst, peer):
        i = len(sent)
        cp = pltpu.make_async_remote_copy(
            src_ref=src, dst_ref=dst, send_sem=ssem.at[i], recv_sem=rsem.at[i],
            device_id=peer, device_id_type=MESH,
        )
        cp.start()
        sent.append(cp)
        return cp

    def share(which, row, rows, col, cols, peer):
        ref = both.at[which, pl.ds(pl.multiple_of(row, 16), rows), pl.ds(pl.multiple_of(col, 128), cols)]
        return send(ref, ref, peer)

    ALL, TK, DY = slice(0, 2), slice(0, 1), slice(1, 2)
    base = c * HALF
    other = 1 - h
    sib = at(c=1 - c)

    def row(yy, hh):
        return (hh * 4 + yy) * 64

    right_x, left_x = at(x=turn(x, 1)), at(x=turn(x, -1))
    right_y, left_y = at(y=turn(y, 1)), at(y=turn(y, -1))
    ym, yp, yo = turn(y, -1), turn(y, 1), turn(y, 2)
    strip = 16 * x

    loads[0].wait()
    loads[1].wait()

    z0 = share(ALL, row(y, h) + strip, 16, base, HALF, at(h=other))

    def y_first(hh, width):
        return (
            share(ALL, row(y, hh) + strip, 16, base + width, HALF - width, right_y),
            share(ALL, row(y, hh) + strip, 16, base + width, HALF - width, left_y),
        )

    def y_block(hh, width):
        return (
            share(ALL, row(y, hh), 64, base, width, right_y),
            share(ALL, row(y, hh), 64, base, width, left_y),
        )

    def x_strip(yy, hh, col, cols):
        r = row(yy, hh) + strip
        return (
            share(ALL, r, 16, base + col, cols, right_x),
            share(ALL, r, 16, base + col, cols, left_x),
        )

    def x_on(yy, hh, col, cols, got):
        got[0].wait_recv()
        a = share(TK, row(yy, hh) + 16 * turn(x, -1), 16, base + col, cols, right_x)
        got[1].wait_recv()
        b = share(DY, row(yy, hh) + 16 * turn(x, 1), 16, base + col, cols, left_x)
        return a, b

    def arrived(pair):
        pair[0].wait_recv()
        pair[1].wait_recv()

    def to_sibling(yy, hh):
        return share(ALL, row(yy, hh), 64, base, HALF, sib)

    def strips_on(hh, width, got):
        got[0].wait_recv()
        a = share(TK, row(ym, hh) + strip, 16, base + width, HALF - width, right_y)
        xa = x_strip(ym, hh, width, HALF - width)
        got[1].wait_recv()
        b = share(DY, row(yp, hh) + strip, 16, base + width, HALF - width, left_y)
        xb = x_strip(yp, hh, width, HALF - width)
        return (a, b), xa, xb

    def blocks_on(hh, width, got):
        got[0].wait_recv()
        a = share(TK, row(ym, hh), 64, base, width, right_y)
        got[1].wait_recv()
        b = share(DY, row(yp, hh), 64, base, width, left_y)
        return a, b

    yb = y_first(h, P2O)
    ya = y_block(h, P2O)

    yb2, xa1, xa2 = strips_on(h, P2O, yb)
    ya2 = blocks_on(h, P2O, ya)
    arrived(yb2)
    xa3 = x_strip(yo, h, P2O, HALF - P2O)
    xf1 = x_on(ym, h, P2O, HALF - P2O, xa1)
    xf2 = x_on(yp, h, P2O, HALF - P2O, xa2)
    z0.wait_recv()
    pb = y_first(other, P2P)
    zx = x_strip(y, other, 0, HALF)
    xf3 = x_on(yo, h, P2O, HALF - P2O, xa3)
    arrived(ya2)
    arrived(xf1)
    sb1 = to_sibling(ym, h)
    arrived(xf2)
    sb2 = to_sibling(yp, h)
    pb2, px1, px2 = strips_on(other, P2P, pb)
    arrived(xf3)
    sb3 = to_sibling(yo, h)
    zxf = x_on(y, other, 0, HALF, zx)
    loads[2].wait()
    ws = send(
        win.at[pl.ds(pl.multiple_of((1 - c) * HALF, 128), HALF)], win_sib, sib
    )
    loads[3].wait()

    def products(slot, hh):
        r = pl.multiple_of(hh * 256, 256)
        pre = jnp.zeros((256, HID), F32)
        back = jnp.zeros((256, HID), F32)
        for k in range(0, FEAT, 768):
            pre += dot(both[0, pl.ds(r, 256), pl.ds(k, 768)], win[pl.ds(k, 768), :], NN)
        part[slot, 0] = pre
        part16[slot, 0] = pre.astype(BF16)
        for k in range(0, FEAT, 768):
            back += dot(both[1, pl.ds(r, 256), pl.ds(k, 768)], wout[:, pl.ds(k, 768)], NT)
        part[slot, 1] = back
        part16[slot, 1] = back.astype(BF16)

    def scatter(slot, s):
        out = {}
        for j in (3, 2, 1):
            src = part16.at[slot, :, pl.ds(pl.multiple_of(s * 128 + 32 * lane[j], 32), 32)]
            out[j] = send(src, inbox.at[slot * 2 + s, j - 1], at(l=lane[j]))
        return out

    sb1.wait_recv()
    sb2.wait_recv()
    sb3.wait_recv()
    products(0, h)
    rs = {0: scatter(0, 0), 1: scatter(0, 1)}

    arrived(pb2)
    px3 = x_strip(yo, other, P2P, HALF - P2P)
    arrived(zxf)
    pa = y_block(other, P2P)
    sp0 = to_sibling(y, other)
    pf1 = x_on(ym, other, P2P, HALF - P2P, px1)
    pf2 = x_on(yp, other, P2P, HALF - P2P, px2)
    pa2 = blocks_on(other, P2P, pa)
    pf3 = x_on(yo, other, P2P, HALF - P2P, px3)
    arrived(pf1)
    sp1 = to_sibling(ym, other)
    arrived(pf2)
    sp2 = to_sibling(yp, other)

    def rows_of(k):
        hh = h if k < 2 else other
        return hh * 256 + (k % 2) * 128

    def finish_sum(k):
        slot, s = k // 2, k % 2
        for j in (1, 2, 3):
            rs[k][j].wait_recv()
        r = pl.multiple_of(s * 128 + 32 * l, 32)
        pre = part[slot, 0, pl.ds(r, 32)]
        back = part[slot, 1, pl.ds(r, 32)]
        for j in (1, 2, 3):
            pre += inbox[k, j - 1, 0].astype(F32)
            back += inbox[k, j - 1, 1].astype(F32)
        act, dpre = gelu_pair(pre, back)
        q = pl.multiple_of(rows_of(k) + 32 * l, 32)
        acts[0, pl.ds(q, 32)] = act
        acts[1, pl.ds(q, 32)] = dpre
        ref = acts.at[:, pl.ds(q, 32)]
        return send(ref, ref, at(l=l2)), send(ref, ref, at(l=l1))

    def pass_on(k, ag):
        ag[0].wait_recv()
        ref = acts.at[:, pl.ds(pl.multiple_of(rows_of(k) + 32 * l2, 32), 32)]
        return send(ref, ref, at(l=l1))

    def to_pair(k, ag, fw):
        ag[1].wait_recv()
        fw.wait_recv()
        r = pl.ds(pl.multiple_of(rows_of(k), 128), 128)
        return send(acts.at[1, r], dpre_sib.at[r], sib)

    def token_part(k, sd):
        sd.wait_recv()
        r = pl.ds(pl.multiple_of(rows_of(k), 128), 128)
        for col in range(0, HALF, 512):
            w = win[pl.ds(pl.multiple_of(base + col, 128), 512), :]
            q = dot(acts[1, r], w, NT) + dot(dpre_sib[r], win_sib[pl.ds(col, 512), :], NT)
            quad[k, :, :, :, pl.ds(col, 512)] = q.reshape(4, 4, 8, 512)
        out = []
        for j in (2, 1, 3):
            yy = turn(y, j)
            ysend[k, j - 1] = quad[k, :, yy].reshape(32, HALF).astype(BF16)
            out.append(send(ysend.at[k, j - 1], yrecv.at[k, j - 1], at(y=yy)))
        return out

    def x_copy(k, xx):
        j = (xx - x + 4) % 4
        return pltpu.make_async_remote_copy(
            src_ref=xsend.at[k], dst_ref=xrecv.at[j - 1],
            send_sem=xs_sem.at[k], recv_sem=xr_sem.at[j - 1],
            device_id=at(x=xx), device_id_type=MESH,
        )

    def x_dest(k):
        return 2 * (h if k < 2 else other) + k % 2

    def y_sum(k, cy):
        for cp in cy:
            cp.wait_recv()
        total = quad[k, :, y].reshape(32, HALF)
        for j in (1, 2, 3):
            total += yrecv[k, j - 1].astype(F32)
        xx = x_dest(k)

        @pl.when(x == xx)
        def _():
            own[...] = total

        @pl.when(x != xx)
        def _():
            xsend[k] = total.astype(BF16)
            x_copy(k, xx).start()

    ag = {0: finish_sum(0)}
    arrived(pa2)
    arrived(pf3)
    sp3 = to_sibling(yo, other)
    for cp in (sp0, sp1, sp2, sp3):
        cp.wait_recv()
    products(1, other)
    rs[2] = scatter(1, 0)
    rs[3] = scatter(1, 1)
    ws.wait_recv()
    ag[1] = finish_sum(1)
    fw = {0: pass_on(0, ag[0])}
    fw[1] = pass_on(1, ag[1])
    sd = {0: to_pair(0, ag[0], fw[0])}
    cy = {0: token_part(0, sd[0])}
    ag[2] = finish_sum(2)
    sd[1] = to_pair(1, ag[1], fw[1])
    cy[1] = token_part(1, sd[1])
    ag[3] = finish_sum(3)
    fw[2] = pass_on(2, ag[2])
    y_sum(0, cy[0])
    fw[3] = pass_on(3, ag[3])
    sd[2] = to_pair(2, ag[2], fw[2])
    cy[2] = token_part(2, sd[2])
    y_sum(1, cy[1])
    sd[3] = to_pair(3, ag[3], fw[3])
    cy[3] = token_part(3, sd[3])

    def grad_out_tile(i, _):
        col = pl.ds(pl.multiple_of(i * 512, 512), 512)
        gwo[:, col] = dot(acts[0], both[1, :, col], TN).astype(BF16)
        return 0

    def grad_in_tile(i, _):
        col = pl.ds(pl.multiple_of(i * 512, 512), 512)
        gwi[col, :] = dot(both[0, :, col], acts[1], TN).astype(BF16)
        return 0

    lax.fori_loop(0, FEAT // 512, grad_out_tile, 0)
    save_o = pltpu.make_async_copy(gwo, gwo_hbm, lsem.at[4])
    save_o.start()
    y_sum(2, cy[2])
    y_sum(3, cy[3])
    lax.fori_loop(0, FEAT // 512, grad_in_tile, 0)
    save_i = pltpu.make_async_copy(gwi, gwi_hbm, lsem.at[5])
    save_i.start()

    total = own[...]
    for j in (1, 2, 3):
        pltpu.make_async_remote_copy(
            src_ref=xsend.at[0], dst_ref=xrecv.at[j - 1], send_sem=xs_sem.at[0],
            recv_sem=xr_sem.at[j - 1], device_id=at(x=turn(x, j)), device_id_type=MESH,
        ).wait_recv()
        total += xrecv[j - 1].astype(F32)
    fin_send[...] = total.reshape(2, 2, 8, HALF)
    f1 = send(fin_send.at[c, other], fin_recv.at[0], at(h=other))
    f2 = send(fin_send.at[1 - c, other], fin_recv.at[1], at(h=other, c=1 - c))
    f3 = send(fin_send.at[1 - c, h], fin_recv.at[2], sib)
    f1.wait_recv()
    gt_ref[:, pl.ds(pl.multiple_of(base, 128), HALF)] = (
        fin_send[c, h] + fin_recv[0]
    ).astype(BF16)
    f2.wait_recv()
    f3.wait_recv()
    gt_ref[:, pl.ds(pl.multiple_of((1 - c) * HALF, 128), HALF)] = (
        fin_recv[1] + fin_recv[2]
    ).astype(BF16)

    for k in range(4):
        xx = x_dest(k)

        @pl.when(x != xx)
        def _():
            x_copy(k, xx).wait_send()

    for cp in sent:
        cp.wait_send()
    save_o.wait()
    save_i.wait()


def shards(tokens, grad_out, w_in, w_out):
    any_ = pl.BlockSpec(memory_space=pl.ANY)
    vm = pltpu.VMEM
    return pl.pallas_call(
        kernel,
        out_shape=(
            jax.ShapeDtypeStruct((8, FEAT), BF16),
            jax.ShapeDtypeStruct((FEAT, HID), BF16),
            jax.ShapeDtypeStruct((HID, FEAT), BF16),
        ),
        in_specs=[any_] * 4,
        out_specs=(pl.BlockSpec(memory_space=pltpu.VMEM), any_, any_),
        scratch_shapes=[
            vm((2, TOK, FEAT), BF16),
            vm((FEAT, HID), BF16),
            vm((HID, FEAT), BF16),
            vm((HALF, HID), BF16),
            vm((2, 2, 256, HID), F32),
            vm((2, 2, 256, HID), BF16),
            vm((4, 3, 2, 32, HID), BF16),
            vm((2, TOK, HID), BF16),
            vm((TOK, HID), BF16),
            vm((4, 4, 4, 8, HALF), F32),
            vm((4, 3, 32, HALF), BF16),
            vm((4, 3, 32, HALF), BF16),
            vm((4, 32, HALF), BF16),
            vm((3, 32, HALF), BF16),
            vm((32, HALF), F32),
            vm((2, 2, 8, HALF), F32),
            vm((3, 8, HALF), F32),
            vm((FEAT, HID), BF16),
            vm((HID, FEAT), BF16),
            pltpu.SemaphoreType.DMA((N_SEMS,)),
            pltpu.SemaphoreType.DMA((N_SEMS,)),
            pltpu.SemaphoreType.DMA((4,)),
            pltpu.SemaphoreType.DMA((3,)),
            pltpu.SemaphoreType.DMA((6,)),
        ],
        compiler_params=pltpu.CompilerParams(
            collective_id=0, has_side_effects=True, vmem_limit_bytes=44 << 20
        ),
        cost_estimate=pl.CostEstimate(
            flops=6_000_000_000, bytes_accessed=12_000_000, transcendentals=100_000
        ),
        name="ffn_backward",
    )(tokens, grad_out, w_in, w_out)


def solution(mesh):
    placed = (P("gz", "gx"), P("gz", "gx"), P("gx", ("gy", "gz")), P(("gy", "gz"), "gx"))
    return jax.shard_map(
        shards,
        mesh=mesh,
        in_specs=placed,
        out_specs=(P(("gy", "gz"), "gx"), P("gx", ("gy", "gz")), P(("gy", "gz"), "gx")),
        check_vma=False,
    )
```

```python
import functools

import jax
import jax.numpy as jnp
from jax import lax
from jax.experimental import pallas as pl
from jax.experimental.pallas import tpu as pltpu
from jax.sharding import PartitionSpec as P

MESH = pl.DeviceIdType.MESH
F32, BF16 = jnp.float32, jnp.bfloat16
coef = 0.7978845608028654
NN = (((1,), (0,)), ((), ()))
NT = (((1,), (1,)), ((), ()))
TN = (((0,), (0,)), ((), ()))

FEAT, HID, TOK = 3072, 384, 512
HALF = FEAT // 2
P2O, P2P = 768, 512
N_SEMS = 128


def gelu_pair(pre, back):
    inner = coef * (pre + 0.044715 * pre * pre * pre)
    tval = jnp.tanh(inner)
    act = 0.5 * pre * (1.0 + tval)
    slope = 0.5 * (1.0 + tval) + 0.5 * pre * (1.0 - tval * tval) * coef * (
        1.0 + 3.0 * 0.044715 * pre * pre
    )
    return act.astype(BF16), (back * slope).astype(BF16)


def dot(a, b, dims):
    return lax.dot_general(a, b, dims, preferred_element_type=F32)


def kernel(
    tok_hbm, dy_hbm, win_hbm, wout_hbm,
    gt_ref, gwi_hbm, gwo_hbm,
    both, win, wout, win_sib, part, part16, inbox, acts, dpre_sib,
    quad, ysend, yrecv, xsend, xrecv, own, fin_send, fin_recv, gwi, gwo,
    ssem, rsem, xs_sem, xr_sem, lsem,
):
    gx, gy, gz = lax.axis_index("gx"), lax.axis_index("gy"), lax.axis_index("gz")
    x, c, y, h, l = gy // 2, gy % 2, gz % 4, gz // 4, gx

    def at(x=x, c=c, y=y, h=h, l=l):
        return (l, x * 2 + c, h * 4 + y)

    def turn(v, d):
        return (v + d + 4) % 4

    l1, l2, l3 = l + 1 - 2 * (l % 2), turn(l, 2), 3 - l
    lane = {1: l1, 2: l2, 3: l3}

    mine = pl.multiple_of(gz * 64, 64)
    loads = [
        pltpu.make_async_copy(tok_hbm, both.at[0, pl.ds(mine, 64)], lsem.at[0]),
        pltpu.make_async_copy(dy_hbm, both.at[1, pl.ds(mine, 64)], lsem.at[1]),
        pltpu.make_async_copy(win_hbm, win, lsem.at[2]),
        pltpu.make_async_copy(wout_hbm, wout, lsem.at[3]),
    ]
    for cp in loads:
        cp.start()

    peers = (
        [at(x=turn(x, d)) for d in (1, 2, 3)]
        + [at(y=turn(y, d)) for d in (1, 2, 3)]
        + [at(l=lane[j]) for j in (1, 2, 3)]
        + [at(h=1 - h), at(h=1 - h, c=1 - c), at(c=1 - c)]
    )
    barrier = pltpu.get_barrier_semaphore()
    for peer in peers:
        pl.semaphore_signal(barrier, inc=1, device_id=peer, device_id_type=MESH)
    pl.semaphore_wait(barrier, len(peers))

    sent = []

    def send(src, dst, peer):
        i = len(sent)
        cp = pltpu.make_async_remote_copy(
            src_ref=src, dst_ref=dst, send_sem=ssem.at[i], recv_sem=rsem.at[i],
            device_id=peer, device_id_type=MESH,
        )
        cp.start()
        sent.append(cp)
        return cp

    def share(which, row, rows, col, cols, peer):
        ref = both.at[which, pl.ds(pl.multiple_of(row, 16), rows), pl.ds(pl.multiple_of(col, 128), cols)]
        return send(ref, ref, peer)

    ALL = slice(0, 2)
    base = c * HALF
    other = 1 - h
    sib = at(c=1 - c)

    def row(yy, hh):
        return (hh * 4 + yy) * 64

    strip = 16 * x

    loads[0].wait()
    loads[1].wait()

    turns = (1, 3, 2)
    z0 = share(ALL, row(y, h) + strip, 16, base, HALF, at(h=other))

    def to_y(hh, first, rows, col, cols):
        return {
            j: share(ALL, row(y, hh) + first, rows, base + col, cols, at(y=turn(y, j)))
            for j in turns
        }

    def to_x(yy, hh, col, cols):
        r = row(yy, hh) + strip
        return [share(ALL, r, 16, base + col, cols, at(x=turn(x, j))) for j in turns]

    def strips_on(hh, width, got):
        out = {}
        for j in turns:
            got[j].wait_recv()
            out[j] = to_x(turn(y, -j), hh, width, HALF - width)
        return out

    def to_sibling(yy, hh, col, cols):
        return share(ALL, row(yy, hh), 64, base + col, cols, sib)

    def arrived(copies):
        for cp in copies:
            cp.wait_recv()

    def products(pos, pieces):
        n = sum(rows for _, rows in pieces)
        for which, w, dims in ((0, win, NN), (1, wout, NT)):
            total = jnp.zeros((n, HID), F32)
            for k in range(0, FEAT, 768):
                lhs = [
                    both[which, pl.ds(pl.multiple_of(r, 64), rows), pl.ds(k, 768)]
                    for r, rows in pieces
                ]
                lhs = lhs[0] if len(lhs) == 1 else jnp.concatenate(lhs, axis=0)
                rhs = w[pl.ds(k, 768), :] if which == 0 else w[:, pl.ds(k, 768)]
                total += dot(lhs, rhs, dims)
            part[which, pl.ds(pos, n)] = total
            part16[which, pl.ds(pos, n)] = total.astype(BF16)

    chunks = [
        (0, 16, lambda v: row(y, h) + 16 * v),
        (64, 32, lambda v: row(turn(y, 2 * (v // 2) - 1), h) + 32 * (v % 2)),
        (192, 16, lambda v: row(turn(y, 2), h) + 16 * v),
        (256, 32, lambda v: row(0, other) + 32 * v),
        (384, 32, lambda v: row(2, other) + 32 * v),
    ]

    def scatter(k):
        pos, m, _ = chunks[k]
        out = []
        for j in (3, 2, 1):
            src = part16.at[:, pl.ds(pl.multiple_of(pos + m * lane[j], 16), m)]
            out.append(send(src, inbox.at[k, j - 1, :, pl.ds(0, m)], at(l=lane[j])))
        return out

    def share_rows(k, v):
        _, m, first = chunks[k]
        return pl.ds(pl.multiple_of(first(v), 16), m)

    def finish_sum(k):
        pos, m, _ = chunks[k]
        for cp in rs[k]:
            cp.wait_recv()
        r = pl.ds(pl.multiple_of(pos + m * l, 16), m)
        pre, back = part[0, r], part[1, r]
        for j in (1, 2, 3):
            pre += inbox[k, j - 1, 0, 0:m].astype(F32)
            back += inbox[k, j - 1, 1, 0:m].astype(F32)
        act, dpre = gelu_pair(pre, back)
        q = share_rows(k, l)
        acts[0, q] = act
        acts[1, q] = dpre
        ref = acts.at[:, q]
        ag[k] = [send(ref, ref, at(l=l2)), send(ref, ref, at(l=l1))]

    def pass_on(k):
        ag[k][0].wait_recv()
        ref = acts.at[:, share_rows(k, l2)]
        ag[k].append(send(ref, ref, at(l=l1)))

    def gathered(k):
        ag[k][1].wait_recv()
        ag[k][2].wait_recv()

    rs, ag = {}, {}
    yb = to_y(h, strip, 16, P2O, HALF - P2O)
    ya = to_y(h, 0, 64, 0, P2O)
    loads[2].wait()
    loads[3].wait()
    products(0, [(row(y, h), 64)])
    rs[0] = scatter(0)
    xa = strips_on(h, P2O, yb)
    z0.wait_recv()
    zx = to_x(y, other, 0, HALF)
    pb = to_y(other, strip, 16, P2P, HALF - P2P)
    finish_sum(0)
    ws = send(
        win.at[pl.ds(pl.multiple_of((1 - c) * HALF, 128), HALF)], win_sib, sib
    )
    got = []
    for j in (1, 3):
        ya[j].wait_recv()
        got.append(to_sibling(turn(y, -j), h, 0, P2O))
    for j in (1, 3):
        arrived(xa[j])
        got.append(to_sibling(turn(y, -j), h, P2O, HALF - P2O))
    pass_on(0)
    arrived(got)
    products(64, [(row(turn(y, -1), h), 64), (row(turn(y, 1), h), 64)])
    rs[1] = scatter(1)
    ya[2].wait_recv()
    got = [to_sibling(turn(y, 2), h, 0, P2O)]
    arrived(xa[2])
    got.append(to_sibling(turn(y, 2), h, P2O, HALF - P2O))
    px = strips_on(other, P2P, pb)
    arrived(got)
    products(192, [(row(turn(y, 2), h), 64)])
    rs[2] = scatter(2)
    arrived(zx)
    pa = to_y(other, 0, 64, 0, P2P)
    got = [to_sibling(y, other, 0, HALF)]
    finish_sum(1)
    gathered(0)
    for j in turns:
        arrived(px[j])
        got.append(to_sibling(turn(y, -j), other, P2P, HALF - P2P))
    finish_sum(2)
    pass_on(1)
    for j in turns:
        pa[j].wait_recv()
        got.append(to_sibling(turn(y, -j), other, 0, P2P))
    arrived(got)
    products(256, [(row(0, other), 256)])
    rs[3] = scatter(3)
    rs[4] = scatter(4)
    pass_on(2)
    ws.wait_recv()

    def rows_of(k):
        hh = h if k < 2 else other
        return hh * 256 + (k % 2) * 128

    def to_pair(k):
        r = pl.ds(pl.multiple_of(rows_of(k), 128), 128)
        return send(acts.at[1, r], dpre_sib.at[r], sib)

    def token_part(k, sd):
        sd.wait_recv()
        r = pl.ds(pl.multiple_of(rows_of(k), 128), 128)
        for col in range(0, HALF, 512):
            w = win[pl.ds(pl.multiple_of(base + col, 128), 512), :]
            q = dot(acts[1, r], w, NT) + dot(dpre_sib[r], win_sib[pl.ds(col, 512), :], NT)
            quad[k, :, :, :, pl.ds(col, 512)] = q.reshape(4, 4, 8, 512)
        out = []
        for j in (2, 1, 3):
            yy = turn(y, j)
            ysend[k, j - 1] = quad[k, :, yy].reshape(32, HALF).astype(BF16)
            out.append(send(ysend.at[k, j - 1], yrecv.at[k, j - 1], at(y=yy)))
        return out

    def x_copy(k, xx):
        j = (xx - x + 4) % 4
        return pltpu.make_async_remote_copy(
            src_ref=xsend.at[k], dst_ref=xrecv.at[j - 1],
            send_sem=xs_sem.at[k], recv_sem=xr_sem.at[j - 1],
            device_id=at(x=xx), device_id_type=MESH,
        )

    def x_dest(k):
        return 2 * (h if k < 2 else other) + k % 2

    def y_sum(k, cy):
        for cp in cy:
            cp.wait_recv()
        total = quad[k, :, y].reshape(32, HALF)
        for j in (1, 2, 3):
            total += yrecv[k, j - 1].astype(F32)
        xx = x_dest(k)

        @pl.when(x == xx)
        def _():
            own[...] = total

        @pl.when(x != xx)
        def _():
            xsend[k] = total.astype(BF16)
            x_copy(k, xx).start()

    gathered(1)
    gathered(2)
    sd = {0: to_pair(0), 1: to_pair(1)}
    cy = {0: token_part(0, sd[0])}
    cy[1] = token_part(1, sd[1])
    finish_sum(3)
    pass_on(3)
    finish_sum(4)
    y_sum(0, cy[0])
    y_sum(1, cy[1])
    gathered(3)
    sd[2] = to_pair(2)
    pass_on(4)
    cy[2] = token_part(2, sd[2])
    gathered(4)
    sd[3] = to_pair(3)
    cy[3] = token_part(3, sd[3])

    def grad_out_tile(i, _):
        col = pl.ds(pl.multiple_of(i * 512, 512), 512)
        gwo[:, col] = dot(acts[0], both[1, :, col], TN).astype(BF16)
        return 0

    def grad_in_tile(i, _):
        col = pl.ds(pl.multiple_of(i * 512, 512), 512)
        gwi[col, :] = dot(both[0, :, col], acts[1], TN).astype(BF16)
        return 0

    lax.fori_loop(0, FEAT // 512, grad_out_tile, 0)
    save_o = pltpu.make_async_copy(gwo, gwo_hbm, lsem.at[4])
    save_o.start()
    y_sum(2, cy[2])
    y_sum(3, cy[3])
    lax.fori_loop(0, FEAT // 512, grad_in_tile, 0)
    save_i = pltpu.make_async_copy(gwi, gwi_hbm, lsem.at[5])
    save_i.start()

    total = own[...]
    for j in (1, 2, 3):
        pltpu.make_async_remote_copy(
            src_ref=xsend.at[0], dst_ref=xrecv.at[j - 1], send_sem=xs_sem.at[0],
            recv_sem=xr_sem.at[j - 1], device_id=at(x=turn(x, j)), device_id_type=MESH,
        ).wait_recv()
        total += xrecv[j - 1].astype(F32)
    fin_send[...] = total.reshape(2, 2, 8, HALF)
    f1 = send(fin_send.at[c, other], fin_recv.at[0], at(h=other))
    f2 = send(fin_send.at[1 - c, other], fin_recv.at[1], at(h=other, c=1 - c))
    f3 = send(fin_send.at[1 - c, h], fin_recv.at[2], sib)
    f1.wait_recv()
    gt_ref[:, pl.ds(pl.multiple_of(base, 128), HALF)] = (
        fin_send[c, h] + fin_recv[0]
    ).astype(BF16)
    f2.wait_recv()
    f3.wait_recv()
    gt_ref[:, pl.ds(pl.multiple_of((1 - c) * HALF, 128), HALF)] = (
        fin_recv[1] + fin_recv[2]
    ).astype(BF16)

    for k in range(4):
        xx = x_dest(k)

        @pl.when(x != xx)
        def _():
            x_copy(k, xx).wait_send()

    for cp in sent:
        cp.wait_send()
    save_o.wait()
    save_i.wait()


def shards(tokens, grad_out, w_in, w_out):
    any_ = pl.BlockSpec(memory_space=pl.ANY)
    vm = pltpu.VMEM
    return pl.pallas_call(
        kernel,
        out_shape=(
            jax.ShapeDtypeStruct((8, FEAT), BF16),
            jax.ShapeDtypeStruct((FEAT, HID), BF16),
            jax.ShapeDtypeStruct((HID, FEAT), BF16),
        ),
        in_specs=[any_] * 4,
        out_specs=(pl.BlockSpec(memory_space=pltpu.VMEM), any_, any_),
        scratch_shapes=[
            vm((2, TOK, FEAT), BF16),
            vm((FEAT, HID), BF16),
            vm((HID, FEAT), BF16),
            vm((HALF, HID), BF16),
            vm((2, TOK, HID), F32),
            vm((2, TOK, HID), BF16),
            vm((5, 3, 2, 32, HID), BF16),
            vm((2, TOK, HID), BF16),
            vm((TOK, HID), BF16),
            vm((4, 4, 4, 8, HALF), F32),
            vm((4, 3, 32, HALF), BF16),
            vm((4, 3, 32, HALF), BF16),
            vm((4, 32, HALF), BF16),
            vm((3, 32, HALF), BF16),
            vm((32, HALF), F32),
            vm((2, 2, 8, HALF), F32),
            vm((3, 8, HALF), F32),
            vm((FEAT, HID), BF16),
            vm((HID, FEAT), BF16),
            pltpu.SemaphoreType.DMA((N_SEMS,)),
            pltpu.SemaphoreType.DMA((N_SEMS,)),
            pltpu.SemaphoreType.DMA((4,)),
            pltpu.SemaphoreType.DMA((3,)),
            pltpu.SemaphoreType.DMA((6,)),
        ],
        compiler_params=pltpu.CompilerParams(
            collective_id=0, has_side_effects=True, vmem_limit_bytes=56 << 20
        ),
        cost_estimate=pl.CostEstimate(
            flops=6_000_000_000, bytes_accessed=12_000_000, transcendentals=100_000
        ),
        name="ffn_backward",
    )(tokens, grad_out, w_in, w_out)


def solution(mesh):
    placed = (P("gz", "gx"), P("gz", "gx"), P("gx", ("gy", "gz")), P(("gy", "gz"), "gx"))
    return jax.shard_map(
        shards,
        mesh=mesh,
        in_specs=placed,
        out_specs=(P(("gy", "gz"), "gx"), P("gx", ("gy", "gz")), P(("gy", "gz"), "gx")),
        check_vma=False,
    )
```

```python
import functools

import jax
import jax.numpy as jnp
from jax import lax
from jax.experimental import pallas as pl
from jax.experimental.pallas import tpu as pltpu
from jax.sharding import PartitionSpec as P

MESH = pl.DeviceIdType.MESH
F32, BF16 = jnp.float32, jnp.bfloat16
coef = 0.7978845608028654
NN = (((1,), (0,)), ((), ()))
NT = (((1,), (1,)), ((), ()))
TN = (((0,), (0,)), ((), ()))

FEAT, HID, TOK = 3072, 384, 512
HALF = FEAT // 2
P2O, P2P = 768, 512
N_SEMS = 128


def gelu_pair(pre, back):
    inner = coef * (pre + 0.044715 * pre * pre * pre)
    tval = jnp.tanh(inner)
    act = 0.5 * pre * (1.0 + tval)
    slope = 0.5 * (1.0 + tval) + 0.5 * pre * (1.0 - tval * tval) * coef * (
        1.0 + 3.0 * 0.044715 * pre * pre
    )
    return act.astype(BF16), (back * slope).astype(BF16)


def dot(a, b, dims):
    return lax.dot_general(a, b, dims, preferred_element_type=F32)


def kernel(
    tok_hbm, dy_hbm, win_hbm, wout_hbm,
    gt_ref, gwi_hbm, gwo_hbm,
    both, win, wout, win_sib, part, part16, inbox, acts, dpre_sib,
    quad, ysend, yrecv, xsend, xrecv, own, fin_send, fin_recv, gwi, gwo,
    ssem, rsem, xs_sem, xr_sem, fs_sem, fr_sem, lsem,
):
    gx, gy, gz = lax.axis_index("gx"), lax.axis_index("gy"), lax.axis_index("gz")
    x, c, y, h, l = gy // 2, gy % 2, gz % 4, gz // 4, gx

    def at(x=x, c=c, y=y, h=h, l=l):
        return (l, x * 2 + c, h * 4 + y)

    def turn(v, d):
        return (v + d + 4) % 4

    l1, l2, l3 = l + 1 - 2 * (l % 2), turn(l, 2), 3 - l
    lane = {1: l1, 2: l2, 3: l3}

    mine = pl.multiple_of(gz * 64, 64)
    loads = [
        pltpu.make_async_copy(tok_hbm, both.at[0, pl.ds(mine, 64)], lsem.at[0]),
        pltpu.make_async_copy(dy_hbm, both.at[1, pl.ds(mine, 64)], lsem.at[1]),
        pltpu.make_async_copy(win_hbm, win, lsem.at[2]),
        pltpu.make_async_copy(wout_hbm, wout, lsem.at[3]),
    ]
    for cp in loads:
        cp.start()

    peers = (
        [at(x=turn(x, d)) for d in (1, 2, 3)]
        + [at(y=turn(y, d)) for d in (1, 2, 3)]
        + [at(l=lane[j]) for j in (1, 2, 3)]
        + [at(h=1 - h), at(h=1 - h, c=1 - c), at(c=1 - c)]
    )
    barrier = pltpu.get_barrier_semaphore()
    for peer in peers:
        pl.semaphore_signal(barrier, inc=1, device_id=peer, device_id_type=MESH)
    pl.semaphore_wait(barrier, len(peers))

    sent = []

    def send(src, dst, peer):
        i = len(sent)
        cp = pltpu.make_async_remote_copy(
            src_ref=src, dst_ref=dst, send_sem=ssem.at[i], recv_sem=rsem.at[i],
            device_id=peer, device_id_type=MESH,
        )
        cp.start()
        sent.append(cp)
        return cp

    def share(which, row, rows, col, cols, peer):
        ref = both.at[which, pl.ds(pl.multiple_of(row, 16), rows), pl.ds(pl.multiple_of(col, 128), cols)]
        return send(ref, ref, peer)

    ALL = slice(0, 2)
    base = c * HALF
    other = 1 - h
    sib = at(c=1 - c)

    def row(yy, hh):
        return (hh * 4 + yy) * 64

    strip = 16 * x

    loads[0].wait()
    loads[1].wait()

    turns = (1, 3, 2)
    z0 = share(ALL, row(y, h) + strip, 16, base, HALF, at(h=other))

    def to_y(hh, first, rows, col, cols):
        return {
            j: share(ALL, row(y, hh) + first, rows, base + col, cols, at(y=turn(y, j)))
            for j in turns
        }

    def to_x(yy, hh, col, cols):
        r = row(yy, hh) + strip
        return [share(ALL, r, 16, base + col, cols, at(x=turn(x, j))) for j in turns]

    def strips_on(hh, width, got):
        out = {}
        for j in turns:
            got[j].wait_recv()
            out[j] = to_x(turn(y, -j), hh, width, HALF - width)
        return out

    def to_sibling(yy, hh, col, cols):
        return share(ALL, row(yy, hh), 64, base + col, cols, sib)

    def arrived(copies):
        for cp in copies:
            cp.wait_recv()

    def products(pos, pieces):
        n = sum(rows for _, rows in pieces)
        for which, w, dims in ((0, win, NN), (1, wout, NT)):
            total = jnp.zeros((n, HID), F32)
            for k in range(0, FEAT, 768):
                lhs = [
                    both[which, pl.ds(pl.multiple_of(r, 64), rows), pl.ds(k, 768)]
                    for r, rows in pieces
                ]
                lhs = lhs[0] if len(lhs) == 1 else jnp.concatenate(lhs, axis=0)
                rhs = w[pl.ds(k, 768), :] if which == 0 else w[:, pl.ds(k, 768)]
                total += dot(lhs, rhs, dims)
            part[which, pl.ds(pos, n)] = total
            part16[which, pl.ds(pos, n)] = total.astype(BF16)

    chunks = [
        (0, 16, lambda v: row(y, h) + 16 * v),
        (64, 32, lambda v: row(turn(y, 2 * (v // 2) - 1), h) + 32 * (v % 2)),
        (192, 16, lambda v: row(turn(y, 2), h) + 16 * v),
        (256, 32, lambda v: row(2 * (v // 2), other) + 32 * (v % 2)),
        (384, 32, lambda v: row(2 * (v // 2) + 1, other) + 32 * (v % 2)),
    ]

    def scatter(k):
        pos, m, _ = chunks[k]
        out = []
        for j in (3, 2, 1):
            src = part16.at[:, pl.ds(pl.multiple_of(pos + m * lane[j], 16), m)]
            out.append(send(src, inbox.at[k, j - 1, :, pl.ds(0, m)], at(l=lane[j])))
        return out

    def share_rows(k, v):
        _, m, first = chunks[k]
        return pl.ds(pl.multiple_of(first(v), 16), m)

    def finish_sum(k):
        pos, m, _ = chunks[k]
        for cp in rs[k]:
            cp.wait_recv()
        r = pl.ds(pl.multiple_of(pos + m * l, 16), m)
        pre, back = part[0, r], part[1, r]
        for j in (1, 2, 3):
            pre += inbox[k, j - 1, 0, 0:m].astype(F32)
            back += inbox[k, j - 1, 1, 0:m].astype(F32)
        act, dpre = gelu_pair(pre, back)
        q = share_rows(k, l)
        acts[0, q] = act
        acts[1, q] = dpre
        ref = acts.at[:, q]
        ag[k] = [send(ref, ref, at(l=l2)), send(ref, ref, at(l=l1))]

    def pass_on(k):
        ag[k][0].wait_recv()
        ref = acts.at[:, share_rows(k, l2)]
        ag[k].append(send(ref, ref, at(l=l1)))

    def gathered(k):
        ag[k][1].wait_recv()
        ag[k][2].wait_recv()

    rs, ag = {}, {}
    yb = to_y(h, strip, 16, P2O, HALF - P2O)
    ya = to_y(h, 0, 64, 0, P2O)
    loads[2].wait()
    loads[3].wait()
    products(0, [(row(y, h), 64)])
    rs[0] = scatter(0)
    xa = strips_on(h, P2O, yb)
    z0.wait_recv()
    zx = to_x(y, other, 0, HALF)
    pb = to_y(other, strip, 16, P2P, HALF - P2P)
    finish_sum(0)
    ws = send(
        win.at[pl.ds(pl.multiple_of((1 - c) * HALF, 128), HALF)], win_sib, sib
    )
    got = []
    for j in (1, 3):
        ya[j].wait_recv()
        got.append(to_sibling(turn(y, -j), h, 0, P2O))
    for j in (1, 3):
        arrived(xa[j])
        got.append(to_sibling(turn(y, -j), h, P2O, HALF - P2O))
    pass_on(0)
    arrived(got)
    products(64, [(row(turn(y, -1), h), 64), (row(turn(y, 1), h), 64)])
    rs[1] = scatter(1)
    ya[2].wait_recv()
    got = [to_sibling(turn(y, 2), h, 0, P2O)]
    arrived(xa[2])
    got.append(to_sibling(turn(y, 2), h, P2O, HALF - P2O))
    px = strips_on(other, P2P, pb)
    arrived(got)
    products(192, [(row(turn(y, 2), h), 64)])
    rs[2] = scatter(2)
    arrived(zx)
    pa = to_y(other, 0, 64, 0, P2P)
    got = [to_sibling(y, other, 0, HALF)]
    finish_sum(1)
    gathered(0)
    for j in turns:
        arrived(px[j])
        got.append(to_sibling(turn(y, -j), other, P2P, HALF - P2P))
    for j in turns:
        pa[j].wait_recv()
        got.append(to_sibling(turn(y, -j), other, 0, P2P))
    finish_sum(2)
    pass_on(1)
    arrived(got)
    products(256, [(row(b, other), 64) for b in (0, 2, 1, 3)])
    rs[3] = scatter(3)
    rs[4] = scatter(4)
    pass_on(2)
    gathered(1)
    ws.wait_recv()

    def half_of(k):
        return h if k < 2 else other

    def blocks_of(k):
        return [
            pl.ds(pl.multiple_of(row(k % 2 + 2 * i, half_of(k)), 64), 64) for i in range(2)
        ]

    def to_pair(k):
        return [send(acts.at[1, r], dpre_sib.at[r], sib) for r in blocks_of(k)]

    def token_part(k, sd):
        arrived(sd)
        mine = jnp.concatenate([acts[1, r] for r in blocks_of(k)], axis=0)
        his = jnp.concatenate([dpre_sib[r] for r in blocks_of(k)], axis=0)
        for col in range(0, HALF, 512):
            w = win[pl.ds(pl.multiple_of(base + col, 128), 512), :]
            q = dot(mine, w, NT) + dot(his, win_sib[pl.ds(col, 512), :], NT)
            quad[k, :, :, :, pl.ds(col, 512)] = q.reshape(4, 4, 8, 512)
        out = []
        for j in (2, 1, 3):
            yy = turn(y, j)
            ysend[k, j - 1] = quad[k, :, yy].reshape(32, HALF).astype(BF16)
            out.append(send(ysend.at[k, j - 1], yrecv.at[k, j - 1], at(y=yy)))
        return out

    def x_copy(k, i):
        xx = 2 * half_of(k) + i
        j = (xx - x + 4) % 4
        return xx, pltpu.make_async_remote_copy(
            src_ref=xsend.at[k, i], dst_ref=xrecv.at[k % 2, j - 1],
            send_sem=xs_sem.at[k, i], recv_sem=xr_sem.at[k % 2, j - 1],
            device_id=at(x=xx), device_id_type=MESH,
        )

    def y_sum(k, cy):
        arrived(cy)
        total = quad[k, :, y].reshape(32, HALF)
        for j in (1, 2, 3):
            total += yrecv[k, j - 1].astype(F32)
        for i in range(2):
            xx, cp = x_copy(k, i)
            piece = total[16 * i : 16 * i + 16]

            @pl.when(x == xx)
            def _(piece=piece):
                own[k % 2] = piece

            @pl.when(x != xx)
            def _(piece=piece, cp=cp):
                xsend[k, i] = piece.astype(BF16)
                cp.start()

    gathered(2)
    sd = {0: to_pair(0), 1: to_pair(1)}
    cy = {0: token_part(0, sd[0])}
    finish_sum(3)
    cy[1] = token_part(1, sd[1])
    finish_sum(4)
    pass_on(3)
    pass_on(4)
    gathered(3)
    sd[2] = to_pair(2)
    cy[2] = token_part(2, sd[2])
    gathered(4)
    sd[3] = to_pair(3)
    y_sum(0, cy[0])
    cy[3] = token_part(3, sd[3])
    y_sum(1, cy[1])

    def grad_out_tile(i, _):
        col = pl.ds(pl.multiple_of(i * 512, 512), 512)
        gwo[:, col] = dot(acts[0], both[1, :, col], TN).astype(BF16)
        return 0

    def grad_in_tile(i, _):
        col = pl.ds(pl.multiple_of(i * 512, 512), 512)
        gwi[col, :] = dot(both[0, :, col], acts[1], TN).astype(BF16)
        return 0

    lax.fori_loop(0, FEAT // 512, grad_out_tile, 0)
    save_o = pltpu.make_async_copy(gwo, gwo_hbm, lsem.at[4])
    save_o.start()
    y_sum(2, cy[2])
    y_sum(3, cy[3])
    lax.fori_loop(0, FEAT // 512, grad_in_tile, 0)
    save_i = pltpu.make_async_copy(gwi, gwi_hbm, lsem.at[5])
    save_i.start()

    last = []
    for core in range(2):
        total = own[core]
        for j in (1, 2, 3):
            pltpu.make_async_remote_copy(
                src_ref=xsend.at[0, 0], dst_ref=xrecv.at[core, j - 1],
                send_sem=xs_sem.at[0, 0], recv_sem=xr_sem.at[core, j - 1],
                device_id=at(x=turn(x, j)), device_id_type=MESH,
            ).wait_recv()
            total += xrecv[core, j - 1].astype(F32)
        fin_send[core] = total.reshape(2, 8, HALF)
        slot = (c + core) % 2
        cp = pltpu.make_async_remote_copy(
            src_ref=fin_send.at[core, other], dst_ref=fin_recv.at[slot],
            send_sem=fs_sem.at[core], recv_sem=fr_sem.at[slot],
            device_id=at(h=other, c=core), device_id_type=MESH,
        )
        cp.start()
        last.append(cp)
    cp = pltpu.make_async_remote_copy(
        src_ref=fin_send.at[1 - c, h], dst_ref=fin_recv.at[2],
        send_sem=fs_sem.at[2], recv_sem=fr_sem.at[2],
        device_id=sib, device_id_type=MESH,
    )
    cp.start()
    last.append(cp)
    for i in range(3):
        pltpu.make_async_remote_copy(
            src_ref=fin_send.at[0, 0], dst_ref=fin_recv.at[i],
            send_sem=fs_sem.at[i], recv_sem=fr_sem.at[i],
            device_id=sib, device_id_type=MESH,
        ).wait_recv()
    gt_ref[:, pl.ds(pl.multiple_of(base, 128), HALF)] = (
        fin_send[c, h] + fin_recv[0]
    ).astype(BF16)
    gt_ref[:, pl.ds(pl.multiple_of((1 - c) * HALF, 128), HALF)] = (
        fin_recv[1] + fin_recv[2]
    ).astype(BF16)

    for cp in last:
        cp.wait_send()
    for k in range(4):
        for i in range(2):
            xx, cp = x_copy(k, i)

            @pl.when(x != xx)
            def _(cp=cp):
                cp.wait_send()

    for cp in sent:
        cp.wait_send()
    save_o.wait()
    save_i.wait()


def place(gt, gwi, gwo, gt_out, gwi_out, gwo_out, gt_vm, gwi_vm, gwo_vm, in_sem, out_sem):
    pieces = []
    for i in range(4):
        r = pl.ds(i * (FEAT // 4), FEAT // 4)
        pieces.append((gwi.at[r], gwi_vm.at[r], gwi_out.at[r]))
        r = pl.ds(i * (HID // 4), HID // 4)
        pieces.append((gwo.at[r], gwo_vm.at[r], gwo_out.at[r]))
    pieces.append((gt, gt_vm, gt_out))
    into = [
        pltpu.make_async_copy(src, mid, in_sem.at[i]) for i, (src, mid, _) in enumerate(pieces)
    ]
    out = [
        pltpu.make_async_copy(mid, dst, out_sem.at[i]) for i, (_, mid, dst) in enumerate(pieces)
    ]
    for cp in into:
        cp.start()
    for a, b in zip(into, out):
        a.wait()
        b.start()
    for cp in out:
        cp.wait()


def shards(tokens, grad_out, w_in, w_out):
    any_ = pl.BlockSpec(memory_space=pl.ANY)
    vm = pltpu.VMEM
    grads = pl.pallas_call(
        kernel,
        out_shape=(
            jax.ShapeDtypeStruct((8, FEAT), BF16),
            jax.ShapeDtypeStruct((FEAT, HID), BF16),
            jax.ShapeDtypeStruct((HID, FEAT), BF16),
        ),
        in_specs=[any_] * 4,
        out_specs=(pl.BlockSpec(memory_space=pltpu.VMEM), any_, any_),
        scratch_shapes=[
            vm((2, TOK, FEAT), BF16),
            vm((FEAT, HID), BF16),
            vm((HID, FEAT), BF16),
            vm((HALF, HID), BF16),
            vm((2, TOK, HID), F32),
            vm((2, TOK, HID), BF16),
            vm((5, 3, 2, 32, HID), BF16),
            vm((2, TOK, HID), BF16),
            vm((TOK, HID), BF16),
            vm((4, 4, 4, 8, HALF), F32),
            vm((4, 3, 32, HALF), BF16),
            vm((4, 3, 32, HALF), BF16),
            vm((4, 2, 16, HALF), BF16),
            vm((2, 3, 16, HALF), BF16),
            vm((2, 16, HALF), F32),
            vm((2, 2, 8, HALF), F32),
            vm((3, 8, HALF), F32),
            vm((FEAT, HID), BF16),
            vm((HID, FEAT), BF16),
            pltpu.SemaphoreType.DMA((N_SEMS,)),
            pltpu.SemaphoreType.DMA((N_SEMS,)),
            pltpu.SemaphoreType.DMA((4, 2)),
            pltpu.SemaphoreType.DMA((2, 3)),
            pltpu.SemaphoreType.DMA((3,)),
            pltpu.SemaphoreType.DMA((3,)),
            pltpu.SemaphoreType.DMA((6,)),
        ],
        compiler_params=pltpu.CompilerParams(
            collective_id=0, has_side_effects=True, vmem_limit_bytes=56 << 20
        ),
        cost_estimate=pl.CostEstimate(
            flops=6_000_000_000, bytes_accessed=12_000_000, transcendentals=100_000
        ),
        name="ffn_backward",
    )(tokens, grad_out, w_in, w_out)
    return pl.pallas_call(
        place,
        out_shape=tuple(jax.ShapeDtypeStruct(g.shape, g.dtype) for g in grads),
        in_specs=[any_] * 3,
        out_specs=(any_,) * 3,
        scratch_shapes=[
            vm((8, FEAT), BF16),
            vm((FEAT, HID), BF16),
            vm((HID, FEAT), BF16),
            pltpu.SemaphoreType.DMA((9,)),
            pltpu.SemaphoreType.DMA((9,)),
        ],
        compiler_params=pltpu.CompilerParams(vmem_limit_bytes=60 << 20),
        name="place",
    )(*grads)


def solution(mesh):
    placed = (P("gz", "gx"), P("gz", "gx"), P("gx", ("gy", "gz")), P(("gy", "gz"), "gx"))
    return jax.shard_map(
        shards,
        mesh=mesh,
        in_specs=placed,
        out_specs=(P(("gy", "gz"), "gx"), P("gx", ("gy", "gz")), P(("gy", "gz"), "gx")),
        check_vma=False,
    )
```

```python
import functools

import jax
import jax.numpy as jnp
from jax import lax
from jax.experimental import pallas as pl
from jax.experimental.pallas import tpu as pltpu
from jax.sharding import PartitionSpec as P

MESH = pl.DeviceIdType.MESH
F32, BF16 = jnp.float32, jnp.bfloat16
coef = 0.7978845608028654
NN = (((1,), (0,)), ((), ()))
NT = (((1,), (1,)), ((), ()))
TN = (((0,), (0,)), ((), ()))

FEAT, HID, TOK = 3072, 384, 512
HALF = FEAT // 2
P2O, P2P = 768, 512
N_SEMS = 160
YF = 1024


def gelu_pair(pre, back):
    inner = coef * (pre + 0.044715 * pre * pre * pre)
    tval = jnp.tanh(inner)
    act = 0.5 * pre * (1.0 + tval)
    slope = 0.5 * (1.0 + tval) + 0.5 * pre * (1.0 - tval * tval) * coef * (
        1.0 + 3.0 * 0.044715 * pre * pre
    )
    return act.astype(BF16), (back * slope).astype(BF16)


def dot(a, b, dims):
    return lax.dot_general(a, b, dims, preferred_element_type=F32)


def kernel(
    tok_hbm, dy_hbm, win_hbm, wout_hbm,
    gt_ref, gwi_hbm, gwo_hbm,
    both, win, wout, win_sib, part, part16, inbox, acts, dpre_sib,
    quad, ysend, yrecv, xsend, xrecv, own, fin_send, fin_recv, gwi, gwo,
    zsend, zrecv, wsend, wrecv, ztot,
    ssem, rsem, xs_sem, xr_sem, fs_sem, fr_sem, zs_sem, zr_sem, ws_sem, wr_sem, lsem,
):
    gx, gy, gz = lax.axis_index("gx"), lax.axis_index("gy"), lax.axis_index("gz")
    x, c, y, h, l = gy // 2, gy % 2, gz % 4, gz // 4, gx

    def at(x=x, c=c, y=y, h=h, l=l):
        return (l, x * 2 + c, h * 4 + y)

    def turn(v, d):
        return (v + d + 4) % 4

    l1, l2, l3 = l + 1 - 2 * (l % 2), turn(l, 2), 3 - l
    lane = {1: l1, 2: l2, 3: l3}

    mine = pl.multiple_of(gz * 64, 64)
    loads = [
        pltpu.make_async_copy(tok_hbm, both.at[0, pl.ds(mine, 64)], lsem.at[0]),
        pltpu.make_async_copy(dy_hbm, both.at[1, pl.ds(mine, 64)], lsem.at[1]),
        pltpu.make_async_copy(win_hbm, win, lsem.at[2]),
        pltpu.make_async_copy(wout_hbm, wout, lsem.at[3]),
    ]
    for cp in loads:
        cp.start()

    peers = (
        [at(x=turn(x, d)) for d in (1, 2, 3)]
        + [at(y=turn(y, d)) for d in (1, 2, 3)]
        + [at(l=lane[j]) for j in (1, 2, 3)]
        + [at(h=1 - h), at(h=1 - h, c=1 - c), at(c=1 - c)]
    )
    barrier = pltpu.get_barrier_semaphore()
    for peer in peers:
        pl.semaphore_signal(barrier, inc=1, device_id=peer, device_id_type=MESH)
    pl.semaphore_wait(barrier, len(peers))

    sent = []

    def send(src, dst, peer):
        i = len(sent)
        cp = pltpu.make_async_remote_copy(
            src_ref=src, dst_ref=dst, send_sem=ssem.at[i], recv_sem=rsem.at[i],
            device_id=peer, device_id_type=MESH,
        )
        cp.start()
        sent.append(cp)
        return cp

    def share(which, row, rows, col, cols, peer):
        ref = both.at[which, pl.ds(pl.multiple_of(row, 16), rows), pl.ds(pl.multiple_of(col, 128), cols)]
        return send(ref, ref, peer)

    ALL = slice(0, 2)
    base = c * HALF
    other = 1 - h
    sib = at(c=1 - c)

    def row(yy, hh):
        return (hh * 4 + yy) * 64

    strip = 16 * x

    loads[0].wait()
    loads[1].wait()

    turns = (1, 3, 2)
    z0 = share(ALL, row(y, h) + strip, 16, base, HALF, at(h=other))

    def to_y(hh, first, rows, col, cols):
        return {
            j: share(ALL, row(y, hh) + first, rows, base + col, cols, at(y=turn(y, j)))
            for j in turns
        }

    def to_x(yy, hh, col, cols):
        r = row(yy, hh) + strip
        return [share(ALL, r, 16, base + col, cols, at(x=turn(x, j))) for j in turns]

    def strips_on(hh, width, got):
        out = {}
        for j in turns:
            got[j].wait_recv()
            out[j] = to_x(turn(y, -j), hh, width, HALF - width)
        return out

    def to_sibling(yy, hh, col, cols):
        return share(ALL, row(yy, hh), 64, base + col, cols, sib)

    def arrived(copies):
        for cp in copies:
            cp.wait_recv()

    def products(pos, pieces):
        n = sum(rows for _, rows in pieces)
        for which, w, dims in ((0, win, NN), (1, wout, NT)):
            total = jnp.zeros((n, HID), F32)
            for k in range(0, FEAT, 768):
                lhs = [
                    both[which, pl.ds(pl.multiple_of(r, 64), rows), pl.ds(k, 768)]
                    for r, rows in pieces
                ]
                lhs = lhs[0] if len(lhs) == 1 else jnp.concatenate(lhs, axis=0)
                rhs = w[pl.ds(k, 768), :] if which == 0 else w[:, pl.ds(k, 768)]
                total += dot(lhs, rhs, dims)
            part[which, pl.ds(pos, n)] = total
            part16[which, pl.ds(pos, n)] = total.astype(BF16)

    late = (turn(y, 2 - 3 * (y % 2)), turn(y, 2 * (y % 2) - 1), turn(y, 1 + y % 2))

    chunks = [
        (0, 16, lambda v: row(y, h) + 16 * v),
        (64, 32, lambda v: row(turn(y, 2 * (v // 2) - 1), h) + 32 * (v % 2)),
        (192, 16, lambda v: row(turn(y, 2), h) + 16 * v),
        (256, 16, lambda v: row(y, other) + 16 * v),
        (320, 16, lambda v: row(late[0], other) + 16 * v),
        (384, 16, lambda v: row(late[1], other) + 16 * v),
        (448, 16, lambda v: row(late[2], other) + 16 * v),
    ]

    def scatter(k):
        pos, m, _ = chunks[k]
        out = []
        for j in (3, 2, 1):
            src = part16.at[:, pl.ds(pl.multiple_of(pos + m * lane[j], 16), m)]
            out.append(send(src, inbox.at[k, j - 1, :, pl.ds(0, m)], at(l=lane[j])))
        return out

    def share_rows(k, v):
        _, m, first = chunks[k]
        return pl.ds(pl.multiple_of(first(v), 16), m)

    def finish_sum(k):
        pos, m, _ = chunks[k]
        for cp in rs[k]:
            cp.wait_recv()
        r = pl.ds(pl.multiple_of(pos + m * l, 16), m)
        pre, back = part[0, r], part[1, r]
        for j in (1, 2, 3):
            pre += inbox[k, j - 1, 0, 0:m].astype(F32)
            back += inbox[k, j - 1, 1, 0:m].astype(F32)
        act, dpre = gelu_pair(pre, back)
        q = share_rows(k, l)
        acts[0, q] = act
        acts[1, q] = dpre
        ref = acts.at[:, q]
        ag[k] = [send(ref, ref, at(l=l2)), send(ref, ref, at(l=l1))]

    def pass_on(k):
        ag[k][0].wait_recv()
        ref = acts.at[:, share_rows(k, l2)]
        ag[k].append(send(ref, ref, at(l=l1)))

    def gathered(k):
        ag[k][1].wait_recv()
        ag[k][2].wait_recv()

    rs, ag = {}, {}
    yb = to_y(h, strip, 16, P2O, HALF - P2O)
    ya = to_y(h, 0, 64, 0, P2O)
    loads[2].wait()
    loads[3].wait()
    products(0, [(row(y, h), 64)])
    rs[0] = scatter(0)
    xa = strips_on(h, P2O, yb)
    z0.wait_recv()
    zx = to_x(y, other, 0, HALF)
    pb = to_y(other, strip, 16, P2P, HALF - P2P)
    finish_sum(0)
    ws = send(
        win.at[pl.ds(pl.multiple_of((1 - c) * HALF, 128), HALF)], win_sib, sib
    )
    got = []
    for j in (1, 3):
        ya[j].wait_recv()
        got.append(to_sibling(turn(y, -j), h, 0, P2O))
    for j in (1, 3):
        arrived(xa[j])
        got.append(to_sibling(turn(y, -j), h, P2O, HALF - P2O))
    pass_on(0)
    arrived(got)
    products(64, [(row(turn(y, -1), h), 64), (row(turn(y, 1), h), 64)])
    rs[1] = scatter(1)
    ya[2].wait_recv()
    got = [to_sibling(turn(y, 2), h, 0, P2O)]
    arrived(xa[2])
    got.append(to_sibling(turn(y, 2), h, P2O, HALF - P2O))
    px = strips_on(other, P2P, pb)
    arrived(got)
    products(192, [(row(turn(y, 2), h), 64)])
    rs[2] = scatter(2)
    arrived(zx)
    pa = to_y(other, 0, 64, 0, P2P)
    near = to_sibling(y, other, 0, HALF)
    got = []
    finish_sum(1)
    near.wait_recv()
    products(256, [(row(y, other), 64)])
    rs[3] = scatter(3)
    gathered(0)
    for j in turns:
        arrived(px[j])
        got.append(to_sibling(turn(y, -j), other, P2P, HALF - P2P))
    for j in turns:
        pa[j].wait_recv()
        got.append(to_sibling(turn(y, -j), other, 0, P2P))
    finish_sum(2)
    pass_on(1)
    finish_sum(3)
    arrived(got)
    products(320, [(row(b, other), 64) for b in late])
    for k in (4, 5, 6):
        rs[k] = scatter(k)
    pass_on(2)
    pass_on(3)
    gathered(1)
    ws.wait_recv()

    def half_of(k):
        return h if k < 2 else other

    def blocks_of(k):
        return [
            pl.ds(pl.multiple_of(row(k % 2 + 2 * i, half_of(k)), 64), 64) for i in range(2)
        ]

    def to_pair(k):
        return [send(acts.at[1, r], dpre_sib.at[r], sib) for r in blocks_of(k)]

    def token_part(k, sd):
        arrived(sd)
        mine = jnp.concatenate([acts[1, r] for r in blocks_of(k)], axis=0)
        his = jnp.concatenate([dpre_sib[r] for r in blocks_of(k)], axis=0)
        for col in range(0, HALF, 512):
            w = win[pl.ds(pl.multiple_of(base + col, 128), 512), :]
            q = dot(mine, w, NT) + dot(his, win_sib[pl.ds(col, 512), :], NT)
            quad[k, :, :, :, pl.ds(col, 512)] = q.reshape(4, 4, 8, 512)
        out = []
        n = cols_of(k)
        for j in (2, 1, 3):
            yy = turn(y, j)
            ysend[k, j - 1, :, 0:n] = quad[k, :, yy, :, 0:n].reshape(32, n).astype(BF16)
            out.append(send(
                ysend.at[k, j - 1, :, pl.ds(0, n)], yrecv.at[k, j - 1, :, pl.ds(0, n)], at(y=yy)
            ))
        if k >= 2:
            for i in range(2):
                xx, cp = z_copy(k, i)

                @pl.when(x != xx)
                def _(i=i, cp=cp):
                    zsend[k - 2, i] = (
                        quad[k, 2 * i : 2 * i + 2, :, :, YF:HALF].reshape(64, HALF - YF).astype(BF16)
                    )
                    cp.start()
        return out

    def z_copy(k, i):
        xx = 2 * half_of(k) + i
        j = (xx - x + 4) % 4
        return xx, pltpu.make_async_remote_copy(
            src_ref=zsend.at[k - 2, i], dst_ref=zrecv.at[k - 2, j - 1],
            send_sem=zs_sem.at[k - 2, i], recv_sem=zr_sem.at[k - 2, j - 1],
            device_id=at(x=xx), device_id_type=MESH,
        )

    def w_copy(k, j):
        return pltpu.make_async_remote_copy(
            src_ref=wsend.at[k - 2, j - 1], dst_ref=wrecv.at[k - 2, j - 1],
            send_sem=ws_sem.at[k - 2, j - 1], recv_sem=wr_sem.at[k - 2, j - 1],
            device_id=at(y=turn(y, j)), device_id_type=MESH,
        )

    def x_sum(k):
        @pl.when(x // 2 == other)
        def _():
            total = quad[k, pl.ds(2 * (x % 2), 2), :, :, YF:HALF]
            for j in (1, 2, 3):
                pltpu.make_async_remote_copy(
                    src_ref=zsend.at[0, 0], dst_ref=zrecv.at[k - 2, j - 1],
                    send_sem=zs_sem.at[0, 0], recv_sem=zr_sem.at[k - 2, j - 1],
                    device_id=at(x=turn(x, j)), device_id_type=MESH,
                ).wait_recv()
                total += zrecv[k - 2, j - 1].astype(F32).reshape(2, 4, 8, HALF - YF)
            ztot[...] = total
            for j in (2, 1, 3):
                wsend[k - 2, j - 1] = (
                    ztot[:, turn(y, j)].reshape(16, HALF - YF).astype(BF16)
                )
                w_copy(k, j).start()
            own[k - 2, :, YF:HALF] = ztot[:, y].reshape(16, HALF - YF)

    def cols_of(k):
        return HALF if k < 2 else YF

    def x_copy(k, i):
        xx = 2 * half_of(k) + i
        j = (xx - x + 4) % 4
        return xx, pltpu.make_async_remote_copy(
            src_ref=xsend.at[k, i, :, pl.ds(0, cols_of(k))],
            dst_ref=xrecv.at[k % 2, j - 1, :, pl.ds(0, cols_of(k))],
            send_sem=xs_sem.at[k, i], recv_sem=xr_sem.at[k % 2, j - 1],
            device_id=at(x=xx), device_id_type=MESH,
        )

    def y_sum(k, cy):
        arrived(cy)
        n = cols_of(k)
        total = quad[k, :, y, :, 0:n].reshape(32, n)
        for j in (1, 2, 3):
            total += yrecv[k, j - 1, :, 0:n].astype(F32)
        for i in range(2):
            xx, cp = x_copy(k, i)
            piece = total[16 * i : 16 * i + 16]

            @pl.when(x == xx)
            def _(piece=piece):
                own[k % 2, :, 0:n] = piece

            @pl.when(x != xx)
            def _(piece=piece, cp=cp):
                xsend[k, i, :, 0:n] = piece.astype(BF16)
                cp.start()

    gathered(2)
    sd = {0: to_pair(0), 1: to_pair(1)}
    cy = {0: token_part(0, sd[0])}
    finish_sum(4)
    finish_sum(5)
    cy[1] = token_part(1, sd[1])
    finish_sum(6)
    pass_on(4)
    pass_on(5)
    pass_on(6)
    gathered(3)
    gathered(4)
    gathered(5)
    sd[2] = to_pair(2)
    cy[2] = token_part(2, sd[2])
    gathered(6)
    sd[3] = to_pair(3)
    y_sum(0, cy[0])
    cy[3] = token_part(3, sd[3])
    y_sum(1, cy[1])

    def grad_out_tile(i, _):
        col = pl.ds(pl.multiple_of(i * 512, 512), 512)
        gwo[:, col] = dot(acts[0], both[1, :, col], TN).astype(BF16)
        return 0

    def grad_in_tile(i, _):
        col = pl.ds(pl.multiple_of(i * 512, 512), 512)
        gwi[col, :] = dot(both[0, :, col], acts[1], TN).astype(BF16)
        return 0

    lax.fori_loop(0, FEAT // 512, grad_out_tile, 0)
    save_o = pltpu.make_async_copy(gwo, gwo_hbm, lsem.at[4])
    save_o.start()
    y_sum(2, cy[2])
    x_sum(2)
    y_sum(3, cy[3])
    x_sum(3)
    lax.fori_loop(0, FEAT // 512, grad_in_tile, 0)
    save_i = pltpu.make_async_copy(gwi, gwi_hbm, lsem.at[5])
    save_i.start()

    last = []
    for core in range(2):
        def from_x(core, n):
            total = own[core, :, 0:n]
            for j in (1, 2, 3):
                pltpu.make_async_remote_copy(
                    src_ref=xsend.at[0, 0, :, pl.ds(0, n)],
                    dst_ref=xrecv.at[core, j - 1, :, pl.ds(0, n)],
                    send_sem=xs_sem.at[0, 0], recv_sem=xr_sem.at[core, j - 1],
                    device_id=at(x=turn(x, j)), device_id_type=MESH,
                ).wait_recv()
                total += xrecv[core, j - 1, :, 0:n].astype(F32)
            fin_send[core, :, :, 0:n] = total.reshape(2, 8, n)

        @pl.when(x // 2 == h)
        def _(core=core):
            from_x(core, HALF)

        @pl.when(x // 2 == other)
        def _(core=core):
            from_x(core, YF)
            total = own[core, :, YF:HALF]
            for j in (1, 2, 3):
                w_copy(core + 2, j).wait_recv()
                total += wrecv[core, j - 1].astype(F32)
            fin_send[core, :, :, YF:HALF] = total.reshape(2, 8, HALF - YF)

        slot = (c + core) % 2
        cp = pltpu.make_async_remote_copy(
            src_ref=fin_send.at[core, other], dst_ref=fin_recv.at[slot],
            send_sem=fs_sem.at[core], recv_sem=fr_sem.at[slot],
            device_id=at(h=other, c=core), device_id_type=MESH,
        )
        cp.start()
        last.append(cp)
    cp = pltpu.make_async_remote_copy(
        src_ref=fin_send.at[1 - c, h], dst_ref=fin_recv.at[2],
        send_sem=fs_sem.at[2], recv_sem=fr_sem.at[2],
        device_id=sib, device_id_type=MESH,
    )
    cp.start()
    last.append(cp)
    for i in range(3):
        pltpu.make_async_remote_copy(
            src_ref=fin_send.at[0, 0], dst_ref=fin_recv.at[i],
            send_sem=fs_sem.at[i], recv_sem=fr_sem.at[i],
            device_id=sib, device_id_type=MESH,
        ).wait_recv()
    gt_ref[:, pl.ds(pl.multiple_of(base, 128), HALF)] = (
        fin_send[c, h] + fin_recv[0]
    ).astype(BF16)
    gt_ref[:, pl.ds(pl.multiple_of((1 - c) * HALF, 128), HALF)] = (
        fin_recv[1] + fin_recv[2]
    ).astype(BF16)

    for cp in last:
        cp.wait_send()
    for k in range(4):
        for i in range(2):
            xx, cp = x_copy(k, i)

            @pl.when(x != xx)
            def _(cp=cp):
                cp.wait_send()

    for k in (2, 3):
        for i in range(2):
            xx, cp = z_copy(k, i)

            @pl.when(x != xx)
            def _(cp=cp):
                cp.wait_send()

        @pl.when(x // 2 == other)
        def _(k=k):
            for j in (1, 2, 3):
                w_copy(k, j).wait_send()

    for cp in sent:
        cp.wait_send()
    save_o.wait()
    save_i.wait()


def place(gt, gwi, gwo, gt_out, gwi_out, gwo_out, gt_vm, gwi_vm, gwo_vm, in_sem, out_sem):
    pieces = []
    for i in range(4):
        r = pl.ds(i * (FEAT // 4), FEAT // 4)
        pieces.append((gwi.at[r], gwi_vm.at[r], gwi_out.at[r]))
        r = pl.ds(i * (HID // 4), HID // 4)
        pieces.append((gwo.at[r], gwo_vm.at[r], gwo_out.at[r]))
    pieces.append((gt, gt_vm, gt_out))
    into = [
        pltpu.make_async_copy(src, mid, in_sem.at[i]) for i, (src, mid, _) in enumerate(pieces)
    ]
    out = [
        pltpu.make_async_copy(mid, dst, out_sem.at[i]) for i, (_, mid, dst) in enumerate(pieces)
    ]
    for cp in into:
        cp.start()
    for a, b in zip(into, out):
        a.wait()
        b.start()
    for cp in out:
        cp.wait()


def shards(tokens, grad_out, w_in, w_out):
    any_ = pl.BlockSpec(memory_space=pl.ANY)
    vm = pltpu.VMEM
    grads = pl.pallas_call(
        kernel,
        out_shape=(
            jax.ShapeDtypeStruct((8, FEAT), BF16),
            jax.ShapeDtypeStruct((FEAT, HID), BF16),
            jax.ShapeDtypeStruct((HID, FEAT), BF16),
        ),
        in_specs=[any_] * 4,
        out_specs=(pl.BlockSpec(memory_space=pltpu.VMEM), any_, any_),
        scratch_shapes=[
            vm((2, TOK, FEAT), BF16),
            vm((FEAT, HID), BF16),
            vm((HID, FEAT), BF16),
            vm((HALF, HID), BF16),
            vm((2, TOK, HID), F32),
            vm((2, TOK, HID), BF16),
            vm((7, 3, 2, 32, HID), BF16),
            vm((2, TOK, HID), BF16),
            vm((TOK, HID), BF16),
            vm((4, 4, 4, 8, HALF), F32),
            vm((4, 3, 32, HALF), BF16),
            vm((4, 3, 32, HALF), BF16),
            vm((4, 2, 16, HALF), BF16),
            vm((2, 3, 16, HALF), BF16),
            vm((2, 16, HALF), F32),
            vm((2, 2, 8, HALF), F32),
            vm((3, 8, HALF), F32),
            vm((FEAT, HID), BF16),
            vm((HID, FEAT), BF16),
            vm((2, 2, 64, HALF - YF), BF16),
            vm((2, 3, 64, HALF - YF), BF16),
            vm((2, 3, 16, HALF - YF), BF16),
            vm((2, 3, 16, HALF - YF), BF16),
            vm((2, 4, 8, HALF - YF), F32),
            pltpu.SemaphoreType.DMA((N_SEMS,)),
            pltpu.SemaphoreType.DMA((N_SEMS,)),
            pltpu.SemaphoreType.DMA((4, 2)),
            pltpu.SemaphoreType.DMA((2, 3)),
            pltpu.SemaphoreType.DMA((3,)),
            pltpu.SemaphoreType.DMA((3,)),
            pltpu.SemaphoreType.DMA((2, 2)),
            pltpu.SemaphoreType.DMA((2, 3)),
            pltpu.SemaphoreType.DMA((2, 3)),
            pltpu.SemaphoreType.DMA((2, 3)),
            pltpu.SemaphoreType.DMA((6,)),
        ],
        compiler_params=pltpu.CompilerParams(
            collective_id=0, has_side_effects=True, vmem_limit_bytes=56 << 20
        ),
        cost_estimate=pl.CostEstimate(
            flops=6_000_000_000, bytes_accessed=12_000_000, transcendentals=100_000
        ),
        name="ffn_backward",
    )(tokens, grad_out, w_in, w_out)
    return pl.pallas_call(
        place,
        out_shape=tuple(jax.ShapeDtypeStruct(g.shape, g.dtype) for g in grads),
        in_specs=[any_] * 3,
        out_specs=(any_,) * 3,
        scratch_shapes=[
            vm((8, FEAT), BF16),
            vm((FEAT, HID), BF16),
            vm((HID, FEAT), BF16),
            pltpu.SemaphoreType.DMA((9,)),
            pltpu.SemaphoreType.DMA((9,)),
        ],
        compiler_params=pltpu.CompilerParams(vmem_limit_bytes=60 << 20),
        name="place",
    )(*grads)


def solution(mesh):
    placed = (P("gz", "gx"), P("gz", "gx"), P("gx", ("gy", "gz")), P(("gy", "gz"), "gx"))
    return jax.shard_map(
        shards,
        mesh=mesh,
        in_specs=placed,
        out_specs=(P(("gy", "gz"), "gx"), P("gx", ("gy", "gz")), P(("gy", "gz"), "gx")),
        check_vma=False,
    )
```

```python
import functools

import jax
import jax.numpy as jnp
from jax import lax
from jax.experimental import pallas as pl
from jax.experimental.pallas import tpu as pltpu
from jax.sharding import PartitionSpec as P

MESH = pl.DeviceIdType.MESH
F32, BF16 = jnp.float32, jnp.bfloat16
coef = 0.7978845608028654
NN = (((1,), (0,)), ((), ()))
NT = (((1,), (1,)), ((), ()))
TN = (((0,), (0,)), ((), ()))

FEAT, HID, TOK = 3072, 384, 512
HALF = FEAT // 2
P2O, P2P = 768, 512
N_SEMS = 160
YF = 1024


def gelu_pair(pre, back):
    inner = coef * (pre + 0.044715 * pre * pre * pre)
    tval = jnp.tanh(inner)
    act = 0.5 * pre * (1.0 + tval)
    slope = 0.5 * (1.0 + tval) + 0.5 * pre * (1.0 - tval * tval) * coef * (
        1.0 + 3.0 * 0.044715 * pre * pre
    )
    return act.astype(BF16), (back * slope).astype(BF16)


def dot(a, b, dims):
    return lax.dot_general(a, b, dims, preferred_element_type=F32)


def kernel(
    tok_hbm, dy_hbm, win_hbm, wout_hbm,
    gt_ref, gwi_hbm, gwo_hbm,
    both, win, wout, win_sib, part, part16, inbox, acts, dpre_sib,
    quad, ysend, yrecv, xsend, xrecv, own, fin_send, fin_recv, gwi, gwo,
    zsend, zrecv, wsend, wrecv, ztot,
    ssem, rsem, xs_sem, xr_sem, fs_sem, fr_sem, zs_sem, zr_sem, ws_sem, wr_sem, lsem,
):
    gx, gy, gz = lax.axis_index("gx"), lax.axis_index("gy"), lax.axis_index("gz")
    x, c, y, h, l = gy // 2, gy % 2, gz % 4, gz // 4, gx

    def at(x=x, c=c, y=y, h=h, l=l):
        return (l, x * 2 + c, h * 4 + y)

    def turn(v, d):
        return (v + d + 4) % 4

    l1, l2, l3 = l + 1 - 2 * (l % 2), turn(l, 2), 3 - l
    lane = {1: l1, 2: l2, 3: l3}

    mine = pl.multiple_of(gz * 64, 64)
    loads = [
        pltpu.make_async_copy(tok_hbm, both.at[0, pl.ds(mine, 64)], lsem.at[0]),
        pltpu.make_async_copy(dy_hbm, both.at[1, pl.ds(mine, 64)], lsem.at[1]),
        pltpu.make_async_copy(win_hbm, win, lsem.at[2]),
        pltpu.make_async_copy(wout_hbm, wout, lsem.at[3]),
    ]
    for cp in loads:
        cp.start()

    peers = (
        [at(x=turn(x, d)) for d in (1, 2, 3)]
        + [at(y=turn(y, d)) for d in (1, 2, 3)]
        + [at(l=lane[j]) for j in (1, 2, 3)]
        + [at(h=1 - h), at(h=1 - h, c=1 - c), at(c=1 - c)]
    )
    barrier = pltpu.get_barrier_semaphore()
    for peer in peers:
        pl.semaphore_signal(barrier, inc=1, device_id=peer, device_id_type=MESH)
    pl.semaphore_wait(barrier, len(peers))

    sent = []

    def send(src, dst, peer):
        i = len(sent)
        cp = pltpu.make_async_remote_copy(
            src_ref=src, dst_ref=dst, send_sem=ssem.at[i], recv_sem=rsem.at[i],
            device_id=peer, device_id_type=MESH,
        )
        cp.start()
        sent.append(cp)
        return cp

    def share(which, row, rows, col, cols, peer):
        ref = both.at[which, pl.ds(pl.multiple_of(row, 16), rows), pl.ds(pl.multiple_of(col, 128), cols)]
        return send(ref, ref, peer)

    ALL = slice(0, 2)
    base = c * HALF
    other = 1 - h
    sib = at(c=1 - c)

    def row(yy, hh):
        return (hh * 4 + yy) * 64

    strip = 16 * x

    loads[0].wait()
    loads[1].wait()

    turns = (1, 3, 2)
    z0 = share(ALL, row(y, h) + strip, 16, base, HALF, at(h=other))

    def to_y(hh, first, rows, col, cols):
        return {
            j: share(ALL, row(y, hh) + first, rows, base + col, cols, at(y=turn(y, j)))
            for j in turns
        }

    def to_x(yy, hh, col, cols):
        r = row(yy, hh) + strip
        return [share(ALL, r, 16, base + col, cols, at(x=turn(x, j))) for j in turns]

    def strips_on(hh, width, got):
        out = {}
        for j in turns:
            got[j].wait_recv()
            out[j] = to_x(turn(y, -j), hh, width, HALF - width)
        return out

    def to_sibling(yy, hh, col, cols):
        return share(ALL, row(yy, hh), 64, base + col, cols, sib)

    def arrived(copies):
        for cp in copies:
            cp.wait_recv()

    def products(pos, pieces):
        n = sum(rows for _, rows in pieces)
        for which, w, dims in ((0, win, NN), (1, wout, NT)):
            total = jnp.zeros((n, HID), F32)
            for k in range(0, FEAT, 768):
                lhs = [
                    both[which, pl.ds(pl.multiple_of(r, 64), rows), pl.ds(k, 768)]
                    for r, rows in pieces
                ]
                lhs = lhs[0] if len(lhs) == 1 else jnp.concatenate(lhs, axis=0)
                rhs = w[pl.ds(k, 768), :] if which == 0 else w[:, pl.ds(k, 768)]
                total += dot(lhs, rhs, dims)
            part[which, pl.ds(pos, n)] = total
            part16[which, pl.ds(pos, n)] = total.astype(BF16)

    late = (turn(y, 2 - 3 * (y % 2)), turn(y, 2 * (y % 2) - 1), turn(y, 1 + y % 2))

    chunks = [
        (0, 16, lambda v: row(y, h) + 16 * v),
        (64, 32, lambda v: row(turn(y, 2 * (v // 2) - 1), h) + 32 * (v % 2)),
        (192, 16, lambda v: row(turn(y, 2), h) + 16 * v),
        (256, 16, lambda v: row(y, other) + 16 * v),
        (320, 16, lambda v: row(late[0], other) + 16 * v),
        (384, 16, lambda v: row(late[1], other) + 16 * v),
        (448, 16, lambda v: row(late[2], other) + 16 * v),
    ]

    def scatter(k):
        pos, m, _ = chunks[k]
        out = []
        for j in (3, 2, 1):
            src = part16.at[:, pl.ds(pl.multiple_of(pos + m * lane[j], 16), m)]
            out.append(send(src, inbox.at[k, j - 1, :, pl.ds(0, m)], at(l=lane[j])))
        return out

    def share_rows(k, v):
        _, m, first = chunks[k]
        return pl.ds(pl.multiple_of(first(v), 16), m)

    def finish_sum(k):
        pos, m, _ = chunks[k]
        for cp in rs[k]:
            cp.wait_recv()
        r = pl.ds(pl.multiple_of(pos + m * l, 16), m)
        pre, back = part[0, r], part[1, r]
        for j in (1, 2, 3):
            pre += inbox[k, j - 1, 0, 0:m].astype(F32)
            back += inbox[k, j - 1, 1, 0:m].astype(F32)
        act, dpre = gelu_pair(pre, back)
        q = share_rows(k, l)
        acts[0, q] = act
        acts[1, q] = dpre
        ref = acts.at[:, q]
        ag[k] = [send(ref, ref, at(l=l2)), send(ref, ref, at(l=l1))]

    def pass_on(k):
        ag[k][0].wait_recv()
        ref = acts.at[:, share_rows(k, l2)]
        ag[k].append(send(ref, ref, at(l=l1)))

    def gathered(k):
        ag[k][1].wait_recv()
        ag[k][2].wait_recv()

    rs, ag = {}, {}
    yb = to_y(h, strip, 16, P2O, HALF - P2O)
    ya = to_y(h, 0, 64, 0, P2O)
    loads[2].wait()
    loads[3].wait()
    products(0, [(row(y, h), 64)])
    rs[0] = scatter(0)
    xa = strips_on(h, P2O, yb)
    z0.wait_recv()
    zx = to_x(y, other, 0, HALF)
    pb = to_y(other, strip, 16, P2P, HALF - P2P)
    finish_sum(0)
    ws = send(
        win.at[pl.ds(pl.multiple_of((1 - c) * HALF, 128), HALF)], win_sib, sib
    )
    got = []
    for j in (1, 3):
        ya[j].wait_recv()
        got.append(to_sibling(turn(y, -j), h, 0, P2O))
    for j in (1, 3):
        arrived(xa[j])
        got.append(to_sibling(turn(y, -j), h, P2O, HALF - P2O))
    pass_on(0)
    arrived(got)
    products(64, [(row(turn(y, -1), h), 64), (row(turn(y, 1), h), 64)])
    rs[1] = scatter(1)
    ya[2].wait_recv()
    got = [to_sibling(turn(y, 2), h, 0, P2O)]
    arrived(xa[2])
    got.append(to_sibling(turn(y, 2), h, P2O, HALF - P2O))
    px = strips_on(other, P2P, pb)
    arrived(got)
    products(192, [(row(turn(y, 2), h), 64)])
    rs[2] = scatter(2)
    arrived(zx)
    pa = to_y(other, 0, 64, 0, P2P)
    near = to_sibling(y, other, 0, HALF)
    got = []
    finish_sum(1)
    near.wait_recv()
    products(256, [(row(y, other), 64)])
    rs[3] = scatter(3)
    gathered(0)
    for j in turns:
        arrived(px[j])
        got.append(to_sibling(turn(y, -j), other, P2P, HALF - P2P))
    for j in turns:
        pa[j].wait_recv()
        got.append(to_sibling(turn(y, -j), other, 0, P2P))
    finish_sum(2)
    pass_on(1)
    finish_sum(3)
    arrived(got)
    products(320, [(row(b, other), 64) for b in late])
    for k in (4, 5, 6):
        rs[k] = scatter(k)
    pass_on(2)
    pass_on(3)
    gathered(1)
    ws.wait_recv()

    def half_of(k):
        return h if k < 2 else other

    def blocks_of(k):
        return [
            pl.ds(pl.multiple_of(row(k % 2 + 2 * i, half_of(k)), 64), 64) for i in range(2)
        ]

    def to_pair(k):
        return [send(acts.at[1, r], dpre_sib.at[r], sib) for r in blocks_of(k)]

    def token_part(k, sd):
        arrived(sd)
        mine = jnp.concatenate([acts[1, r] for r in blocks_of(k)], axis=0)
        his = jnp.concatenate([dpre_sib[r] for r in blocks_of(k)], axis=0)
        for col in range(0, HALF, 512):
            w = win[pl.ds(pl.multiple_of(base + col, 128), 512), :]
            q = dot(mine, w, NT) + dot(his, win_sib[pl.ds(col, 512), :], NT)
            quad[k, :, :, :, pl.ds(col, 512)] = q.reshape(4, 4, 8, 512)
        out = []
        n = cols_of(k)
        for j in (2, 1, 3):
            yy = turn(y, j)
            ysend[k, j - 1, :, 0:n] = quad[k, :, yy, :, 0:n].reshape(32, n).astype(BF16)
            out.append(send(
                ysend.at[k, j - 1, :, pl.ds(0, n)], yrecv.at[k, j - 1, :, pl.ds(0, n)], at(y=yy)
            ))
        if k >= 2:
            for i in range(2):
                xx, cp = z_copy(k, i)

                @pl.when(x != xx)
                def _(i=i, cp=cp):
                    zsend[k - 2, i] = (
                        quad[k, 2 * i : 2 * i + 2, :, :, YF:HALF].reshape(64, HALF - YF).astype(BF16)
                    )
                    cp.start()
        return out

    def z_copy(k, i):
        xx = 2 * half_of(k) + i
        j = (xx - x + 4) % 4
        return xx, pltpu.make_async_remote_copy(
            src_ref=zsend.at[k - 2, i], dst_ref=zrecv.at[k - 2, j - 1],
            send_sem=zs_sem.at[k - 2, i], recv_sem=zr_sem.at[k - 2, j - 1],
            device_id=at(x=xx), device_id_type=MESH,
        )

    def w_copy(k, j):
        return pltpu.make_async_remote_copy(
            src_ref=wsend.at[k - 2, j - 1], dst_ref=wrecv.at[k - 2, j - 1],
            send_sem=ws_sem.at[k - 2, j - 1], recv_sem=wr_sem.at[k - 2, j - 1],
            device_id=at(y=turn(y, j)), device_id_type=MESH,
        )

    def x_sum(k):
        @pl.when(x // 2 == other)
        def _():
            total = quad[k, pl.ds(2 * (x % 2), 2), :, :, YF:HALF]
            for j in (1, 2, 3):
                pltpu.make_async_remote_copy(
                    src_ref=zsend.at[0, 0], dst_ref=zrecv.at[k - 2, j - 1],
                    send_sem=zs_sem.at[0, 0], recv_sem=zr_sem.at[k - 2, j - 1],
                    device_id=at(x=turn(x, j)), device_id_type=MESH,
                ).wait_recv()
                total += zrecv[k - 2, j - 1].astype(F32).reshape(2, 4, 8, HALF - YF)
            ztot[...] = total
            for j in (2, 1, 3):
                wsend[k - 2, j - 1] = (
                    ztot[:, turn(y, j)].reshape(16, HALF - YF).astype(BF16)
                )
                w_copy(k, j).start()
            own[k - 2, :, YF:HALF] = ztot[:, y].reshape(16, HALF - YF)

    def cols_of(k):
        return HALF if k < 2 else YF

    def x_copy(k, i):
        xx = 2 * half_of(k) + i
        j = (xx - x + 4) % 4
        return xx, pltpu.make_async_remote_copy(
            src_ref=xsend.at[k, i, :, pl.ds(0, cols_of(k))],
            dst_ref=xrecv.at[k % 2, j - 1, :, pl.ds(0, cols_of(k))],
            send_sem=xs_sem.at[k, i], recv_sem=xr_sem.at[k % 2, j - 1],
            device_id=at(x=xx), device_id_type=MESH,
        )

    def y_sum(k, cy):
        arrived(cy)
        n = cols_of(k)
        total = quad[k, :, y, :, 0:n].reshape(32, n)
        for j in (1, 2, 3):
            total += yrecv[k, j - 1, :, 0:n].astype(F32)
        for i in range(2):
            xx, cp = x_copy(k, i)
            piece = total[16 * i : 16 * i + 16]

            @pl.when(x == xx)
            def _(piece=piece):
                own[k % 2, :, 0:n] = piece

            @pl.when(x != xx)
            def _(piece=piece, cp=cp):
                xsend[k, i, :, 0:n] = piece.astype(BF16)
                cp.start()

    gathered(2)
    sd = {0: to_pair(0), 1: to_pair(1)}
    cy = {0: token_part(0, sd[0])}
    finish_sum(4)
    finish_sum(5)
    finish_sum(6)
    cy[1] = token_part(1, sd[1])
    pass_on(4)
    pass_on(5)
    pass_on(6)
    gathered(3)
    gathered(4)
    gathered(5)
    sd[2] = to_pair(2)
    cy[2] = token_part(2, sd[2])
    gathered(6)
    sd[3] = to_pair(3)
    cy[3] = token_part(3, sd[3])
    y_sum(0, cy[0])
    y_sum(1, cy[1])

    def grad_out_tile(i, _):
        col = pl.ds(pl.multiple_of(i * 512, 512), 512)
        gwo[:, col] = dot(acts[0], both[1, :, col], TN).astype(BF16)
        return 0

    def grad_in_tile(i, _):
        col = pl.ds(pl.multiple_of(i * 512, 512), 512)
        gwi[col, :] = dot(both[0, :, col], acts[1], TN).astype(BF16)
        return 0

    lax.fori_loop(0, FEAT // 512, grad_out_tile, 0)
    save_o = pltpu.make_async_copy(gwo, gwo_hbm, lsem.at[4])
    save_o.start()
    y_sum(2, cy[2])
    x_sum(2)
    y_sum(3, cy[3])
    x_sum(3)
    lax.fori_loop(0, FEAT // 512, grad_in_tile, 0)
    save_i = pltpu.make_async_copy(gwi, gwi_hbm, lsem.at[5])
    save_i.start()

    last = []
    for core in range(2):
        def from_x(core, n):
            total = own[core, :, 0:n]
            for j in (1, 2, 3):
                pltpu.make_async_remote_copy(
                    src_ref=xsend.at[0, 0, :, pl.ds(0, n)],
                    dst_ref=xrecv.at[core, j - 1, :, pl.ds(0, n)],
                    send_sem=xs_sem.at[0, 0], recv_sem=xr_sem.at[core, j - 1],
                    device_id=at(x=turn(x, j)), device_id_type=MESH,
                ).wait_recv()
                total += xrecv[core, j - 1, :, 0:n].astype(F32)
            fin_send[core, :, :, 0:n] = total.reshape(2, 8, n)

        @pl.when(x // 2 == h)
        def _(core=core):
            from_x(core, HALF)

        @pl.when(x // 2 == other)
        def _(core=core):
            from_x(core, YF)
            total = own[core, :, YF:HALF]
            for j in (1, 2, 3):
                w_copy(core + 2, j).wait_recv()
                total += wrecv[core, j - 1].astype(F32)
            fin_send[core, :, :, YF:HALF] = total.reshape(2, 8, HALF - YF)

        slot = (c + core) % 2
        cp = pltpu.make_async_remote_copy(
            src_ref=fin_send.at[core, other], dst_ref=fin_recv.at[slot],
            send_sem=fs_sem.at[core], recv_sem=fr_sem.at[slot],
            device_id=at(h=other, c=core), device_id_type=MESH,
        )
        cp.start()
        last.append(cp)
    cp = pltpu.make_async_remote_copy(
        src_ref=fin_send.at[1 - c, h], dst_ref=fin_recv.at[2],
        send_sem=fs_sem.at[2], recv_sem=fr_sem.at[2],
        device_id=sib, device_id_type=MESH,
    )
    cp.start()
    last.append(cp)
    for i in range(3):
        pltpu.make_async_remote_copy(
            src_ref=fin_send.at[0, 0], dst_ref=fin_recv.at[i],
            send_sem=fs_sem.at[i], recv_sem=fr_sem.at[i],
            device_id=sib, device_id_type=MESH,
        ).wait_recv()
    gt_ref[:, pl.ds(pl.multiple_of(base, 128), HALF)] = (
        fin_send[c, h] + fin_recv[0]
    ).astype(BF16)
    gt_ref[:, pl.ds(pl.multiple_of((1 - c) * HALF, 128), HALF)] = (
        fin_recv[1] + fin_recv[2]
    ).astype(BF16)

    for cp in last:
        cp.wait_send()
    for k in range(4):
        for i in range(2):
            xx, cp = x_copy(k, i)

            @pl.when(x != xx)
            def _(cp=cp):
                cp.wait_send()

    for k in (2, 3):
        for i in range(2):
            xx, cp = z_copy(k, i)

            @pl.when(x != xx)
            def _(cp=cp):
                cp.wait_send()

        @pl.when(x // 2 == other)
        def _(k=k):
            for j in (1, 2, 3):
                w_copy(k, j).wait_send()

    for cp in sent:
        cp.wait_send()
    save_o.wait()
    save_i.wait()


def place(gt, gwi, gwo, gt_out, gwi_out, gwo_out, gt_vm, gwi_vm, gwo_vm, in_sem, out_sem):
    pieces = []
    for i in range(4):
        r = pl.ds(i * (FEAT // 4), FEAT // 4)
        pieces.append((gwi.at[r], gwi_vm.at[r], gwi_out.at[r]))
        r = pl.ds(i * (HID // 4), HID // 4)
        pieces.append((gwo.at[r], gwo_vm.at[r], gwo_out.at[r]))
    pieces.append((gt, gt_vm, gt_out))
    into = [
        pltpu.make_async_copy(src, mid, in_sem.at[i]) for i, (src, mid, _) in enumerate(pieces)
    ]
    out = [
        pltpu.make_async_copy(mid, dst, out_sem.at[i]) for i, (_, mid, dst) in enumerate(pieces)
    ]
    for cp in into:
        cp.start()
    for a, b in zip(into, out):
        a.wait()
        b.start()
    for cp in out:
        cp.wait()


def shards(tokens, grad_out, w_in, w_out):
    any_ = pl.BlockSpec(memory_space=pl.ANY)
    vm = pltpu.VMEM
    grads = pl.pallas_call(
        kernel,
        out_shape=(
            jax.ShapeDtypeStruct((8, FEAT), BF16),
            jax.ShapeDtypeStruct((FEAT, HID), BF16),
            jax.ShapeDtypeStruct((HID, FEAT), BF16),
        ),
        in_specs=[any_] * 4,
        out_specs=(pl.BlockSpec(memory_space=pltpu.VMEM), any_, any_),
        scratch_shapes=[
            vm((2, TOK, FEAT), BF16),
            vm((FEAT, HID), BF16),
            vm((HID, FEAT), BF16),
            vm((HALF, HID), BF16),
            vm((2, TOK, HID), F32),
            vm((2, TOK, HID), BF16),
            vm((7, 3, 2, 32, HID), BF16),
            vm((2, TOK, HID), BF16),
            vm((TOK, HID), BF16),
            vm((4, 4, 4, 8, HALF), F32),
            vm((4, 3, 32, HALF), BF16),
            vm((4, 3, 32, HALF), BF16),
            vm((4, 2, 16, HALF), BF16),
            vm((2, 3, 16, HALF), BF16),
            vm((2, 16, HALF), F32),
            vm((2, 2, 8, HALF), F32),
            vm((3, 8, HALF), F32),
            vm((FEAT, HID), BF16),
            vm((HID, FEAT), BF16),
            vm((2, 2, 64, HALF - YF), BF16),
            vm((2, 3, 64, HALF - YF), BF16),
            vm((2, 3, 16, HALF - YF), BF16),
            vm((2, 3, 16, HALF - YF), BF16),
            vm((2, 4, 8, HALF - YF), F32),
            pltpu.SemaphoreType.DMA((N_SEMS,)),
            pltpu.SemaphoreType.DMA((N_SEMS,)),
            pltpu.SemaphoreType.DMA((4, 2)),
            pltpu.SemaphoreType.DMA((2, 3)),
            pltpu.SemaphoreType.DMA((3,)),
            pltpu.SemaphoreType.DMA((3,)),
            pltpu.SemaphoreType.DMA((2, 2)),
            pltpu.SemaphoreType.DMA((2, 3)),
            pltpu.SemaphoreType.DMA((2, 3)),
            pltpu.SemaphoreType.DMA((2, 3)),
            pltpu.SemaphoreType.DMA((6,)),
        ],
        compiler_params=pltpu.CompilerParams(
            collective_id=0, has_side_effects=True, vmem_limit_bytes=56 << 20
        ),
        cost_estimate=pl.CostEstimate(
            flops=6_000_000_000, bytes_accessed=12_000_000, transcendentals=100_000
        ),
        name="ffn_backward",
    )(tokens, grad_out, w_in, w_out)
    return pl.pallas_call(
        place,
        out_shape=tuple(jax.ShapeDtypeStruct(g.shape, g.dtype) for g in grads),
        in_specs=[any_] * 3,
        out_specs=(any_,) * 3,
        scratch_shapes=[
            vm((8, FEAT), BF16),
            vm((FEAT, HID), BF16),
            vm((HID, FEAT), BF16),
            pltpu.SemaphoreType.DMA((9,)),
            pltpu.SemaphoreType.DMA((9,)),
        ],
        compiler_params=pltpu.CompilerParams(vmem_limit_bytes=60 << 20),
        name="place",
    )(*grads)


def solution(mesh):
    placed = (P("gz", "gx"), P("gz", "gx"), P("gx", ("gy", "gz")), P(("gy", "gz"), "gx"))
    return jax.shard_map(
        shards,
        mesh=mesh,
        in_specs=placed,
        out_specs=(P(("gy", "gz"), "gx"), P("gx", ("gy", "gz")), P(("gy", "gz"), "gx")),
        check_vma=False,
    )
```

```python
import functools

import jax
import jax.numpy as jnp
from jax import lax
from jax.experimental import pallas as pl
from jax.experimental.pallas import tpu as pltpu
from jax.sharding import PartitionSpec as P

MESH = pl.DeviceIdType.MESH
F32, BF16 = jnp.float32, jnp.bfloat16
coef = 0.7978845608028654
NN = (((1,), (0,)), ((), ()))
NT = (((1,), (1,)), ((), ()))
TN = (((0,), (0,)), ((), ()))

FEAT, HID, TOK = 3072, 384, 512
HALF = FEAT // 2
P2O, P2P = 768, 512
N_SEMS = 160
YF = 1024
DIRECT = (2, 3, 4, 5, 6)


def gelu_pair(pre, back):
    inner = coef * (pre + 0.044715 * pre * pre * pre)
    tval = jnp.tanh(inner)
    act = 0.5 * pre * (1.0 + tval)
    slope = 0.5 * (1.0 + tval) + 0.5 * pre * (1.0 - tval * tval) * coef * (
        1.0 + 3.0 * 0.044715 * pre * pre
    )
    return act.astype(BF16), (back * slope).astype(BF16)


def dot(a, b, dims):
    return lax.dot_general(a, b, dims, preferred_element_type=F32)


def kernel(
    tok_hbm, dy_hbm, win_hbm, wout_hbm,
    gt_ref, gwi_hbm, gwo_hbm,
    both, win, wout, win_sib, part, part16, inbox, acts, dpre_sib,
    quad, ysend, yrecv, xsend, xrecv, own, fin_send, fin_recv, gwi, gwo,
    zsend, zrecv, wsend, wrecv, ztot,
    ssem, rsem, xs_sem, xr_sem, fs_sem, fr_sem, zs_sem, zr_sem, ws_sem, wr_sem, lsem,
):
    gx, gy, gz = lax.axis_index("gx"), lax.axis_index("gy"), lax.axis_index("gz")
    x, c, y, h, l = gy // 2, gy % 2, gz % 4, gz // 4, gx

    def at(x=x, c=c, y=y, h=h, l=l):
        return (l, x * 2 + c, h * 4 + y)

    def turn(v, d):
        return (v + d + 4) % 4

    l1, l2, l3 = l + 1 - 2 * (l % 2), turn(l, 2), 3 - l
    lane = {1: l1, 2: l2, 3: l3}

    mine = pl.multiple_of(gz * 64, 64)
    loads = [
        pltpu.make_async_copy(tok_hbm, both.at[0, pl.ds(mine, 64)], lsem.at[0]),
        pltpu.make_async_copy(dy_hbm, both.at[1, pl.ds(mine, 64)], lsem.at[1]),
        pltpu.make_async_copy(win_hbm, win, lsem.at[2]),
        pltpu.make_async_copy(wout_hbm, wout, lsem.at[3]),
    ]
    for cp in loads:
        cp.start()

    peers = (
        [at(x=turn(x, d)) for d in (1, 2, 3)]
        + [at(y=turn(y, d)) for d in (1, 2, 3)]
        + [at(l=lane[j]) for j in (1, 2, 3)]
        + [at(h=1 - h), at(h=1 - h, c=1 - c), at(c=1 - c)]
    )
    barrier = pltpu.get_barrier_semaphore()
    for peer in peers:
        pl.semaphore_signal(barrier, inc=1, device_id=peer, device_id_type=MESH)
    pl.semaphore_wait(barrier, len(peers))

    sent = []

    def send(src, dst, peer):
        i = len(sent)
        cp = pltpu.make_async_remote_copy(
            src_ref=src, dst_ref=dst, send_sem=ssem.at[i], recv_sem=rsem.at[i],
            device_id=peer, device_id_type=MESH,
        )
        cp.start()
        sent.append(cp)
        return cp

    def share(which, row, rows, col, cols, peer):
        ref = both.at[which, pl.ds(pl.multiple_of(row, 16), rows), pl.ds(pl.multiple_of(col, 128), cols)]
        return send(ref, ref, peer)

    ALL = slice(0, 2)
    base = c * HALF
    other = 1 - h
    sib = at(c=1 - c)

    def row(yy, hh):
        return (hh * 4 + yy) * 64

    strip = 16 * x

    loads[0].wait()
    loads[1].wait()

    turns = (1, 3, 2)
    z0 = share(ALL, row(y, h) + strip, 16, base, HALF, at(h=other))

    def to_y(hh, first, rows, col, cols):
        return {
            j: share(ALL, row(y, hh) + first, rows, base + col, cols, at(y=turn(y, j)))
            for j in turns
        }

    def to_x(yy, hh, col, cols):
        r = row(yy, hh) + strip
        return [share(ALL, r, 16, base + col, cols, at(x=turn(x, j))) for j in turns]

    def strips_on(hh, width, got):
        out = {}
        for j in turns:
            got[j].wait_recv()
            out[j] = to_x(turn(y, -j), hh, width, HALF - width)
        return out

    def to_sibling(yy, hh, col, cols):
        return share(ALL, row(yy, hh), 64, base + col, cols, sib)

    def arrived(copies):
        for cp in copies:
            cp.wait_recv()

    def products(pos, pieces):
        n = sum(rows for _, rows in pieces)
        for which, w, dims in ((0, win, NN), (1, wout, NT)):
            total = jnp.zeros((n, HID), F32)
            for k in range(0, FEAT, 768):
                lhs = [
                    both[which, pl.ds(pl.multiple_of(r, 64), rows), pl.ds(k, 768)]
                    for r, rows in pieces
                ]
                lhs = lhs[0] if len(lhs) == 1 else jnp.concatenate(lhs, axis=0)
                rhs = w[pl.ds(k, 768), :] if which == 0 else w[:, pl.ds(k, 768)]
                total += dot(lhs, rhs, dims)
            part[which, pl.ds(pos, n)] = total
            part16[which, pl.ds(pos, n)] = total.astype(BF16)

    late = (turn(y, 2 - 3 * (y % 2)), turn(y, 2 * (y % 2) - 1), turn(y, 1 + y % 2))

    chunks = [
        (0, 16, lambda v: row(y, h) + 16 * v),
        (64, 32, lambda v: row(turn(y, 2 * (v // 2) - 1), h) + 32 * (v % 2)),
        (192, 16, lambda v: row(turn(y, 2), h) + 16 * v),
        (256, 16, lambda v: row(y, other) + 16 * v),
        (320, 16, lambda v: row(late[0], other) + 16 * v),
        (384, 16, lambda v: row(late[1], other) + 16 * v),
        (448, 16, lambda v: row(late[2], other) + 16 * v),
    ]

    def scatter(k):
        pos, m, _ = chunks[k]
        out = []
        for j in (3, 2, 1):
            src = part16.at[:, pl.ds(pl.multiple_of(pos + m * lane[j], 16), m)]
            out.append(send(src, inbox.at[k, j - 1, :, pl.ds(0, m)], at(l=lane[j])))
        return out

    def share_rows(k, v):
        _, m, first = chunks[k]
        return pl.ds(pl.multiple_of(first(v), 16), m)

    def finish_sum(k):
        pos, m, _ = chunks[k]
        for cp in rs[k]:
            cp.wait_recv()
        r = pl.ds(pl.multiple_of(pos + m * l, 16), m)
        pre, back = part[0, r], part[1, r]
        for j in (1, 2, 3):
            pre += inbox[k, j - 1, 0, 0:m].astype(F32)
            back += inbox[k, j - 1, 1, 0:m].astype(F32)
        act, dpre = gelu_pair(pre, back)
        q = share_rows(k, l)
        acts[0, q] = act
        acts[1, q] = dpre
        ref = acts.at[:, q]
        ag[k] = [send(ref, ref, at(l=l2)), send(ref, ref, at(l=l1))]
        if k in DIRECT:
            ag[k].append(send(ref, ref, at(l=l3)))

    def pass_on(k):
        ag[k][0].wait_recv()
        ref = acts.at[:, share_rows(k, l2)]
        ag[k].append(send(ref, ref, at(l=l1)))

    def gathered(k):
        ag[k][1].wait_recv()
        ag[k][2].wait_recv()
        if k in DIRECT:
            ag[k][0].wait_recv()

    rs, ag = {}, {}
    yb = to_y(h, strip, 16, P2O, HALF - P2O)
    ya = to_y(h, 0, 64, 0, P2O)
    loads[2].wait()
    loads[3].wait()
    products(0, [(row(y, h), 64)])
    rs[0] = scatter(0)
    xa = strips_on(h, P2O, yb)
    z0.wait_recv()
    zx = to_x(y, other, 0, HALF)
    pb = to_y(other, strip, 16, P2P, HALF - P2P)
    finish_sum(0)
    ws = send(
        win.at[pl.ds(pl.multiple_of((1 - c) * HALF, 128), HALF)], win_sib, sib
    )
    got = []
    for j in (1, 3):
        ya[j].wait_recv()
        got.append(to_sibling(turn(y, -j), h, 0, P2O))
    for j in (1, 3):
        arrived(xa[j])
        got.append(to_sibling(turn(y, -j), h, P2O, HALF - P2O))
    pass_on(0)
    arrived(got)
    products(64, [(row(turn(y, -1), h), 64), (row(turn(y, 1), h), 64)])
    rs[1] = scatter(1)
    ya[2].wait_recv()
    got = [to_sibling(turn(y, 2), h, 0, P2O)]
    arrived(xa[2])
    got.append(to_sibling(turn(y, 2), h, P2O, HALF - P2O))
    px = strips_on(other, P2P, pb)
    arrived(got)
    products(192, [(row(turn(y, 2), h), 64)])
    rs[2] = scatter(2)
    arrived(zx)
    pa = to_y(other, 0, 64, 0, P2P)
    near = to_sibling(y, other, 0, HALF)
    got = []
    finish_sum(1)
    near.wait_recv()
    products(256, [(row(y, other), 64)])
    rs[3] = scatter(3)
    gathered(0)
    for j in turns:
        arrived(px[j])
        got.append(to_sibling(turn(y, -j), other, P2P, HALF - P2P))
    for j in turns:
        pa[j].wait_recv()
        got.append(to_sibling(turn(y, -j), other, 0, P2P))
    finish_sum(2)
    pass_on(1)
    finish_sum(3)
    arrived(got)
    products(320, [(row(b, other), 64) for b in late])
    for k in (4, 5, 6):
        rs[k] = scatter(k)
    gathered(1)
    ws.wait_recv()

    def half_of(k):
        return h if k < 2 else other

    def blocks_of(k):
        return [
            pl.ds(pl.multiple_of(row(k % 2 + 2 * i, half_of(k)), 64), 64) for i in range(2)
        ]

    def to_pair(k):
        return [send(acts.at[1, r], dpre_sib.at[r], sib) for r in blocks_of(k)]

    def token_part(k, sd):
        arrived(sd)
        mine = jnp.concatenate([acts[1, r] for r in blocks_of(k)], axis=0)
        his = jnp.concatenate([dpre_sib[r] for r in blocks_of(k)], axis=0)
        for col in range(0, HALF, 512):
            w = win[pl.ds(pl.multiple_of(base + col, 128), 512), :]
            q = dot(mine, w, NT) + dot(his, win_sib[pl.ds(col, 512), :], NT)
            quad[k, :, :, :, pl.ds(col, 512)] = q.reshape(4, 4, 8, 512)
        out = []
        n = cols_of(k)
        for j in (2, 1, 3):
            yy = turn(y, j)
            ysend[k, j - 1, :, 0:n] = quad[k, :, yy, :, 0:n].reshape(32, n).astype(BF16)
            out.append(send(
                ysend.at[k, j - 1, :, pl.ds(0, n)], yrecv.at[k, j - 1, :, pl.ds(0, n)], at(y=yy)
            ))
        if k >= 2:
            for i in range(2):
                xx, cp = z_copy(k, i)

                @pl.when(x != xx)
                def _(i=i, cp=cp):
                    zsend[k - 2, i] = (
                        quad[k, 2 * i : 2 * i + 2, :, :, YF:HALF].reshape(64, HALF - YF).astype(BF16)
                    )
                    cp.start()
        return out

    def z_copy(k, i):
        xx = 2 * half_of(k) + i
        j = (xx - x + 4) % 4
        return xx, pltpu.make_async_remote_copy(
            src_ref=zsend.at[k - 2, i], dst_ref=zrecv.at[k - 2, j - 1],
            send_sem=zs_sem.at[k - 2, i], recv_sem=zr_sem.at[k - 2, j - 1],
            device_id=at(x=xx), device_id_type=MESH,
        )

    def w_copy(k, j):
        return pltpu.make_async_remote_copy(
            src_ref=wsend.at[k - 2, j - 1], dst_ref=wrecv.at[k - 2, j - 1],
            send_sem=ws_sem.at[k - 2, j - 1], recv_sem=wr_sem.at[k - 2, j - 1],
            device_id=at(y=turn(y, j)), device_id_type=MESH,
        )

    def x_sum(k):
        @pl.when(x // 2 == other)
        def _():
            total = quad[k, pl.ds(2 * (x % 2), 2), :, :, YF:HALF]
            for j in (1, 2, 3):
                pltpu.make_async_remote_copy(
                    src_ref=zsend.at[0, 0], dst_ref=zrecv.at[k - 2, j - 1],
                    send_sem=zs_sem.at[0, 0], recv_sem=zr_sem.at[k - 2, j - 1],
                    device_id=at(x=turn(x, j)), device_id_type=MESH,
                ).wait_recv()
                total += zrecv[k - 2, j - 1].astype(F32).reshape(2, 4, 8, HALF - YF)
            ztot[...] = total
            for j in (2, 1, 3):
                wsend[k - 2, j - 1] = (
                    ztot[:, turn(y, j)].reshape(16, HALF - YF).astype(BF16)
                )
                w_copy(k, j).start()
            own[k - 2, :, YF:HALF] = ztot[:, y].reshape(16, HALF - YF)

    def cols_of(k):
        return HALF if k < 2 else YF

    def x_copy(k, i):
        xx = 2 * half_of(k) + i
        j = (xx - x + 4) % 4
        return xx, pltpu.make_async_remote_copy(
            src_ref=xsend.at[k, i, :, pl.ds(0, cols_of(k))],
            dst_ref=xrecv.at[k % 2, j - 1, :, pl.ds(0, cols_of(k))],
            send_sem=xs_sem.at[k, i], recv_sem=xr_sem.at[k % 2, j - 1],
            device_id=at(x=xx), device_id_type=MESH,
        )

    def y_sum(k, cy):
        arrived(cy)
        n = cols_of(k)
        total = quad[k, :, y, :, 0:n].reshape(32, n)
        for j in (1, 2, 3):
            total += yrecv[k, j - 1, :, 0:n].astype(F32)
        for i in range(2):
            xx, cp = x_copy(k, i)
            piece = total[16 * i : 16 * i + 16]

            @pl.when(x == xx)
            def _(piece=piece):
                own[k % 2, :, 0:n] = piece

            @pl.when(x != xx)
            def _(piece=piece, cp=cp):
                xsend[k, i, :, 0:n] = piece.astype(BF16)
                cp.start()

    gathered(2)
    sd = {0: to_pair(0), 1: to_pair(1)}
    cy = {0: token_part(0, sd[0])}
    finish_sum(4)
    finish_sum(5)
    finish_sum(6)
    cy[1] = token_part(1, sd[1])
    gathered(3)
    gathered(4)
    gathered(5)
    sd[2] = to_pair(2)
    cy[2] = token_part(2, sd[2])
    gathered(6)
    sd[3] = to_pair(3)
    cy[3] = token_part(3, sd[3])
    y_sum(0, cy[0])
    y_sum(1, cy[1])

    def grad_out_tile(i, _):
        col = pl.ds(pl.multiple_of(i * 512, 512), 512)
        gwo[:, col] = dot(acts[0], both[1, :, col], TN).astype(BF16)
        return 0

    def grad_in_tile(i, _):
        col = pl.ds(pl.multiple_of(i * 512, 512), 512)
        gwi[col, :] = dot(both[0, :, col], acts[1], TN).astype(BF16)
        return 0

    lax.fori_loop(0, FEAT // 512, grad_out_tile, 0)
    save_o = pltpu.make_async_copy(gwo, gwo_hbm, lsem.at[4])
    save_o.start()
    y_sum(2, cy[2])
    x_sum(2)
    y_sum(3, cy[3])
    x_sum(3)
    lax.fori_loop(0, FEAT // 512, grad_in_tile, 0)
    save_i = pltpu.make_async_copy(gwi, gwi_hbm, lsem.at[5])
    save_i.start()

    last = []
    for core in range(2):
        def from_x(core, n):
            total = own[core, :, 0:n]
            for j in (1, 2, 3):
                pltpu.make_async_remote_copy(
                    src_ref=xsend.at[0, 0, :, pl.ds(0, n)],
                    dst_ref=xrecv.at[core, j - 1, :, pl.ds(0, n)],
                    send_sem=xs_sem.at[0, 0], recv_sem=xr_sem.at[core, j - 1],
                    device_id=at(x=turn(x, j)), device_id_type=MESH,
                ).wait_recv()
                total += xrecv[core, j - 1, :, 0:n].astype(F32)
            fin_send[core, :, :, 0:n] = total.reshape(2, 8, n)

        @pl.when(x // 2 == h)
        def _(core=core):
            from_x(core, HALF)

        @pl.when(x // 2 == other)
        def _(core=core):
            from_x(core, YF)
            total = own[core, :, YF:HALF]
            for j in (1, 2, 3):
                w_copy(core + 2, j).wait_recv()
                total += wrecv[core, j - 1].astype(F32)
            fin_send[core, :, :, YF:HALF] = total.reshape(2, 8, HALF - YF)

        slot = (c + core) % 2
        cp = pltpu.make_async_remote_copy(
            src_ref=fin_send.at[core, other], dst_ref=fin_recv.at[slot],
            send_sem=fs_sem.at[core], recv_sem=fr_sem.at[slot],
            device_id=at(h=other, c=core), device_id_type=MESH,
        )
        cp.start()
        last.append(cp)
    cp = pltpu.make_async_remote_copy(
        src_ref=fin_send.at[1 - c, h], dst_ref=fin_recv.at[2],
        send_sem=fs_sem.at[2], recv_sem=fr_sem.at[2],
        device_id=sib, device_id_type=MESH,
    )
    cp.start()
    last.append(cp)
    for i in range(3):
        pltpu.make_async_remote_copy(
            src_ref=fin_send.at[0, 0], dst_ref=fin_recv.at[i],
            send_sem=fs_sem.at[i], recv_sem=fr_sem.at[i],
            device_id=sib, device_id_type=MESH,
        ).wait_recv()
    gt_ref[:, pl.ds(pl.multiple_of(base, 128), HALF)] = (
        fin_send[c, h] + fin_recv[0]
    ).astype(BF16)
    gt_ref[:, pl.ds(pl.multiple_of((1 - c) * HALF, 128), HALF)] = (
        fin_recv[1] + fin_recv[2]
    ).astype(BF16)

    for cp in last:
        cp.wait_send()
    for k in range(4):
        for i in range(2):
            xx, cp = x_copy(k, i)

            @pl.when(x != xx)
            def _(cp=cp):
                cp.wait_send()

    for k in (2, 3):
        for i in range(2):
            xx, cp = z_copy(k, i)

            @pl.when(x != xx)
            def _(cp=cp):
                cp.wait_send()

        @pl.when(x // 2 == other)
        def _(k=k):
            for j in (1, 2, 3):
                w_copy(k, j).wait_send()

    for cp in sent:
        cp.wait_send()
    save_o.wait()
    save_i.wait()


def place(gt, gwi, gwo, gt_out, gwi_out, gwo_out, gt_vm, gwi_vm, gwo_vm, in_sem, out_sem):
    pieces = []
    for i in range(4):
        r = pl.ds(i * (FEAT // 4), FEAT // 4)
        pieces.append((gwi.at[r], gwi_vm.at[r], gwi_out.at[r]))
        r = pl.ds(i * (HID // 4), HID // 4)
        pieces.append((gwo.at[r], gwo_vm.at[r], gwo_out.at[r]))
    pieces.append((gt, gt_vm, gt_out))
    into = [
        pltpu.make_async_copy(src, mid, in_sem.at[i]) for i, (src, mid, _) in enumerate(pieces)
    ]
    out = [
        pltpu.make_async_copy(mid, dst, out_sem.at[i]) for i, (_, mid, dst) in enumerate(pieces)
    ]
    for cp in into:
        cp.start()
    for a, b in zip(into, out):
        a.wait()
        b.start()
    for cp in out:
        cp.wait()


def shards(tokens, grad_out, w_in, w_out):
    any_ = pl.BlockSpec(memory_space=pl.ANY)
    vm = pltpu.VMEM
    grads = pl.pallas_call(
        kernel,
        out_shape=(
            jax.ShapeDtypeStruct((8, FEAT), BF16),
            jax.ShapeDtypeStruct((FEAT, HID), BF16),
            jax.ShapeDtypeStruct((HID, FEAT), BF16),
        ),
        in_specs=[any_] * 4,
        out_specs=(pl.BlockSpec(memory_space=pltpu.VMEM), any_, any_),
        scratch_shapes=[
            vm((2, TOK, FEAT), BF16),
            vm((FEAT, HID), BF16),
            vm((HID, FEAT), BF16),
            vm((HALF, HID), BF16),
            vm((2, TOK, HID), F32),
            vm((2, TOK, HID), BF16),
            vm((7, 3, 2, 32, HID), BF16),
            vm((2, TOK, HID), BF16),
            vm((TOK, HID), BF16),
            vm((4, 4, 4, 8, HALF), F32),
            vm((4, 3, 32, HALF), BF16),
            vm((4, 3, 32, HALF), BF16),
            vm((4, 2, 16, HALF), BF16),
            vm((2, 3, 16, HALF), BF16),
            vm((2, 16, HALF), F32),
            vm((2, 2, 8, HALF), F32),
            vm((3, 8, HALF), F32),
            vm((FEAT, HID), BF16),
            vm((HID, FEAT), BF16),
            vm((2, 2, 64, HALF - YF), BF16),
            vm((2, 3, 64, HALF - YF), BF16),
            vm((2, 3, 16, HALF - YF), BF16),
            vm((2, 3, 16, HALF - YF), BF16),
            vm((2, 4, 8, HALF - YF), F32),
            pltpu.SemaphoreType.DMA((N_SEMS,)),
            pltpu.SemaphoreType.DMA((N_SEMS,)),
            pltpu.SemaphoreType.DMA((4, 2)),
            pltpu.SemaphoreType.DMA((2, 3)),
            pltpu.SemaphoreType.DMA((3,)),
            pltpu.SemaphoreType.DMA((3,)),
            pltpu.SemaphoreType.DMA((2, 2)),
            pltpu.SemaphoreType.DMA((2, 3)),
            pltpu.SemaphoreType.DMA((2, 3)),
            pltpu.SemaphoreType.DMA((2, 3)),
            pltpu.SemaphoreType.DMA((6,)),
        ],
        compiler_params=pltpu.CompilerParams(
            collective_id=0, has_side_effects=True, vmem_limit_bytes=56 << 20
        ),
        cost_estimate=pl.CostEstimate(
            flops=6_000_000_000, bytes_accessed=12_000_000, transcendentals=100_000
        ),
        name="ffn_backward",
    )(tokens, grad_out, w_in, w_out)
    return pl.pallas_call(
        place,
        out_shape=tuple(jax.ShapeDtypeStruct(g.shape, g.dtype) for g in grads),
        in_specs=[any_] * 3,
        out_specs=(any_,) * 3,
        scratch_shapes=[
            vm((8, FEAT), BF16),
            vm((FEAT, HID), BF16),
            vm((HID, FEAT), BF16),
            pltpu.SemaphoreType.DMA((9,)),
            pltpu.SemaphoreType.DMA((9,)),
        ],
        compiler_params=pltpu.CompilerParams(vmem_limit_bytes=60 << 20),
        name="place",
    )(*grads)


def solution(mesh):
    placed = (P("gz", "gx"), P("gz", "gx"), P("gx", ("gy", "gz")), P(("gy", "gz"), "gx"))
    return jax.shard_map(
        shards,
        mesh=mesh,
        in_specs=placed,
        out_specs=(P(("gy", "gz"), "gx"), P("gx", ("gy", "gz")), P(("gy", "gz"), "gx")),
        check_vma=False,
    )
```
